256 devices in a mesh: lon: 16 (over x_hi, y, core), lev: 16 (over x_lo, z).
Axes of the slice: x: 4 (x_hi: 2, x_lo: 2; x = x_hi * 2 + x_lo), y: 4, z: 8, core: 2. Of those that a mesh axis runs over, the one named last changes fastest.
Arguments:
- inputs: bfloat16 [128, 512, 1024], P('lev', 'lon'), may hold values from -36 to 36
- norm_gain: float32 [1024], replicated, may hold values from 0.25 to 1.75
- w_qkv: bfloat16 [1024, 3072], replicated, may hold values from -0.1875 to 0.1875
- w_out: bfloat16 [1024, 1024], replicated, may hold values from -0.1875 to 0.1875
- d_out: bfloat16 [128, 512, 1024], P('lev', 'lon'), may hold values from -6 to 6
- corner: int32 [128, 512], P('lev', 'lon'), may hold values from 0 to 4
Outputs:
- mixed_out: bfloat16 [128, 512, 1024], P('lev', 'lon')
- grad_input: bfloat16 [128, 512, 1024], P('lev', 'lon')
The draws below stay inside these ranges and needn't reach their ends.
Inputs may be any that keep to these rules, and one draw needn't show every extreme that they name: 0 keeps a cell's whole window; 1 to 4 name the 3 x 3 corner block of offsets that is left out.
All inputs are finite; a program needn't handle non-finite values.
Results may differ from the reference program's by a relative error of at most 0.015.
Values may be sent and summed in bfloat16 or wider, within the bound.
A program may use at most 128 MiB of HBM per device.

```python
import math
import jax
import jax.numpy as jnp
from jax import lax

D = 1024
HEADS = 16
HEAD_DIM = 64
RADIUS = 3
NR = 128
NC = 512


def draw_inputs(key, part):
    key = jax.random.fold_in(key, 17)
    base_key, row_key, col_key = jax.random.split(key, 3)
    base_draw = jax.random.truncated_normal(base_key, -4.0, 4.0, (NR, NC, D), jnp.float32)
    lower_end = 0.3
    upper_end = 3.0
    row_scale = jnp.exp(jax.random.uniform(row_key, (NR, NC, 1), jnp.float32, math.log(lower_end), math.log(upper_end)))
    col_scale = jnp.exp(jax.random.uniform(col_key, (D,), jnp.float32, math.log(lower_end), math.log(upper_end)))
    return (base_draw * row_scale * col_scale).astype(jnp.bfloat16)


def place_ends(entries, stream_key, smallest, largest):
    index_at = [jax.random.randint(jax.random.fold_in(stream_key, axis), (), 0, length) for axis, length in enumerate(entries.shape)]
    widest = entries.shape.index(max(entries.shape))
    beside = index_at[:widest] + [(index_at[widest] + 1) % entries.shape[widest]] + index_at[widest + 1:]
    return entries.at[tuple(index_at)].set(smallest).at[tuple(beside)].set(largest)


def levels(own_key, extent, shards, low, top_value):
    def one(axis_at, parts):
        draws = jax.random.uniform(jax.random.fold_in(jax.random.fold_in(own_key, 6), axis_at), (parts,), jnp.float32, low / len(shards), top_value / len(shards))
        return jnp.repeat(jnp.exp(draws), extent[axis_at] // parts).reshape((-1,) + (1,) * (len(extent) - axis_at - 1))

    factor_of = one(*shards[0])
    for cut in shards[1:]:
        factor_of = factor_of * one(*cut)
    return factor_of


def noise(own_key, dims, deviation, reach, cuts=(), held_as=jnp.bfloat16):
    factor_of = levels(own_key, dims, cuts, -0.22, 0.18) if cuts else 1.0
    entries = jax.random.normal(own_key, dims, jnp.float32) * deviation * factor_of
    return jnp.minimum(jnp.maximum(entries, -reach), reach).astype(held_as)


def setup_inputs(seed: int = 0) -> dict:
    keys = jax.random.split(jax.random.key(seed), 7)
    inputs = draw_inputs(jax.random.fold_in(keys[6], 71), 0)
    norm_gain = jnp.clip(1.0 + 0.15 * jax.random.normal(keys[1], (D,), jnp.float32), 0.25, 1.75)
    w_qkv = noise(keys[2], (D, 3 * D), D ** -0.5, 0.1875)
    w_out = noise(keys[3], (D, D), D ** -0.5, 0.1875)
    d_out = noise(keys[4], (NR, NC, D), 1.0, 6.0, ((0, 16), (1, 16)))
    corner = place_ends(jax.random.randint(keys[5], (NR, NC), 0, 5), jax.random.fold_in(keys[5], 1), 0, 4).astype(jnp.int32)
    return {"inputs": inputs, "norm_gain": norm_gain, "w_qkv": w_qkv, "w_out": w_out, "d_out": d_out, "corner": corner}


EPSILON = 1e-06

def window_offsets():
    return [(row_off, col_off) for row_off in range(-RADIUS, RADIUS + 1) for col_off in range(-RADIUS, RADIUS + 1)]

def shifted(field, row_off, col_off):
    row_count = field.shape[0]
    widths = [(RADIUS, RADIUS)] + [(0, 0)] * (field.ndim - 1)
    padded = jnp.pad(field, widths)
    window = padded[RADIUS + row_off:RADIUS + row_off + row_count]
    return jnp.roll(window, -col_off, axis=1)

def corner_drop(corner, row_off, col_off):
    if row_off < 0 and col_off < 0:
        return corner == 1
    if row_off < 0 and col_off > 0:
        return corner == 2
    if row_off > 0 and col_off < 0:
        return corner == 3
    if row_off > 0 and col_off > 0:
        return corner == 4
    return jnp.zeros(corner.shape, dtype=bool)

def keep_mask(corner, row_off, col_off):
    row_index = jnp.arange(corner.shape[0]) + row_off
    inside = ((row_index >= 0) & (row_index < corner.shape[0]))[:, None]
    return inside & jnp.logical_not(corner_drop(corner, row_off, col_off))

def head_pass(query, key_head, value_head, d_attn, corner):
    score_scale = HEAD_DIM ** (-0.5)
    query_f = query.astype(jnp.float32)
    grad_f = d_attn.astype(jnp.float32)
    pairs = window_offsets()
    exp_terms = []
    for row_off, col_off in pairs:
        key_part = shifted(key_head, row_off, col_off).astype(jnp.float32)
        scores_now = lax.optimization_barrier(jnp.sum(query_f * key_part, axis=-1)) * score_scale
        exp_terms.append(jnp.where(keep_mask(corner, row_off, col_off), jnp.exp(scores_now), 0.0))
    exp_terms = jnp.stack(exp_terms)
    denominator = lax.optimization_barrier(jnp.sum(exp_terms, axis=0))
    weights_f = exp_terms / denominator
    weights_b = lax.optimization_barrier(weights_f.astype(jnp.bfloat16))
    attended = jnp.zeros(query.shape, jnp.float32)
    grad_prob = []
    for offset_idx, (row_off, col_off) in enumerate(pairs):
        value_part = shifted(value_head, row_off, col_off).astype(jnp.float32)
        attended = attended + weights_b[offset_idx].astype(jnp.float32)[..., None] * value_part
        grad_prob.append(lax.optimization_barrier(jnp.sum(grad_f * value_part, axis=-1)))
    grad_prob = jnp.stack(grad_prob)
    row_delta = lax.optimization_barrier(jnp.sum(weights_f * grad_prob, axis=0))
    dscore_b = lax.optimization_barrier((weights_f * (grad_prob - row_delta)).astype(jnp.bfloat16))
    grad_query = jnp.zeros(query.shape, jnp.float32)
    grad_key = jnp.zeros(query.shape, jnp.float32)
    grad_value = jnp.zeros(query.shape, jnp.float32)
    for offset_idx, (row_off, col_off) in enumerate(pairs):
        key_part = shifted(key_head, row_off, col_off).astype(jnp.float32)
        dscore_f = dscore_b[offset_idx].astype(jnp.float32)[..., None]
        grad_query = grad_query + dscore_f * key_part
        grad_key = grad_key + shifted(dscore_f * query_f, -row_off, -col_off)
        weight_now = weights_b[offset_idx].astype(jnp.float32)[..., None]
        grad_value = grad_value + shifted(weight_now * grad_f, -row_off, -col_off)
    return (attended.astype(jnp.bfloat16), (grad_query * score_scale).astype(jnp.bfloat16), (grad_key * score_scale).astype(jnp.bfloat16), grad_value.astype(jnp.bfloat16))

def reference(inputs, norm_gain, w_qkv, w_out, d_out, corner):
    inputs_f = inputs.astype(jnp.float32)
    inv_rms = lax.rsqrt(lax.optimization_barrier(jnp.mean(inputs_f * inputs_f, axis=-1, keepdims=True)) + EPSILON)
    normed = (inputs_f * inv_rms * norm_gain).astype(jnp.bfloat16)
    qkv = jnp.dot(normed.reshape(NR * NC, D), w_qkv, preferred_element_type=jnp.float32).astype(jnp.bfloat16)
    d_attn = jnp.dot(d_out.reshape(NR * NC, D), w_out.T, preferred_element_type=jnp.float32).astype(jnp.bfloat16)

    def split_heads(matrix):
        return matrix.reshape(NR, NC, HEADS, HEAD_DIM).transpose(2, 0, 1, 3)

    def merge_heads(matrix):
        return matrix.transpose(1, 2, 0, 3).reshape(NR * NC, D)
    stacked = (split_heads(qkv[:, :D]), split_heads(qkv[:, D:2 * D]), split_heads(qkv[:, 2 * D:]), split_heads(d_attn))
    attended, grad_query, grad_key, grad_value = lax.map(lambda member: head_pass(member[0], member[1], member[2], member[3], corner), stacked)
    mixed_out = jnp.dot(merge_heads(attended), w_out, preferred_element_type=jnp.float32).astype(jnp.bfloat16)
    grad_qkv = jnp.concatenate([merge_heads(grad_query), merge_heads(grad_key), merge_heads(grad_value)], axis=1)
    d_normed = jnp.dot(grad_qkv, w_qkv.T, preferred_element_type=jnp.float32).reshape(NR, NC, D)
    scaled = d_normed * norm_gain
    grad_input = inv_rms * scaled - inputs_f * inv_rms ** 3 * lax.optimization_barrier(jnp.mean(inputs_f * scaled, axis=-1, keepdims=True))
    return (mixed_out.reshape(NR, NC, D), grad_input.astype(jnp.bfloat16))
```

```python
import jax
import jax.numpy as jnp
import numpy as np
from jax import lax
from jax.experimental import pallas as pl
from jax.experimental.pallas import tpu as pltpu
from jax.sharding import PartitionSpec as P

HEADS = 16
RADIUS = 3
EPSILON = 1e-06

ROWS, COLS, WIDTH = 8, 32, 1024
CELLS = ROWS * COLS
HEAD_DIM = WIDTH // HEADS
QUAD = 4 * HEAD_DIM
QUADS = WIDTH // QUAD
TILE = 8
TILES = COLS // TILE
EXT = ROWS + 2 * RADIUS
SPAN = EXT * 2 * TILE
RIM = RADIUS * COLS
EDGE = EXT * TILE
PACK = 128
HALO = 2 * RIM + PACK
NEG = -1e30

PIECES = (
    ((0, -1), 0, 32),
    ((0, 1), 32, 32),
    ((-1, -1), 64, 16),
    ((-1, 1), 80, 16),
    ((1, -1), 96, 16),
    ((1, 1), 112, 16),
)
AROUND = ((-1, 0), (1, 0)) + tuple(p[0] for p in PIECES)
OPPOSITE = tuple(AROUND.index((-d[0], -d[1])) for d in AROUND)


def selections():
    pack = np.zeros((PACK, CELLS), np.float32)
    spread = np.zeros((EDGE, PACK), np.float32)
    for (up, side), at, _ in PIECES:
        own_rows = {-1: range(RADIUS), 0: range(ROWS), 1: range(ROWS - RADIUS, ROWS)}[up]
        ext_row = {-1: 0, 0: RADIUS, 1: RADIUS + ROWS}[up]
        for i, row in enumerate(own_rows):
            for c in range(RADIUS):
                col = c if side < 0 else COLS - RADIUS + c
                pack[at + i * RADIUS + c, row * COLS + col] = 1
                position = TILE - RADIUS + c if side < 0 else c
                spread[(ext_row + i) * TILE + position, at + i * RADIUS + c] = 1
    return pack, spread


def dot(a, b, dims=((1,), (0,))):
    return lax.dot_general(a, b, (dims, ((), ())), preferred_element_type=jnp.float32)


ROWS_BY_ROWS = ((1,), (1,))
COLS_BY_COLS = ((0,), (0,))


def lanes(index, size=QUAD):
    return pl.ds(pl.multiple_of(index * size, size), size)


def kernel(
    x_hbm, do_hbm, gain_hbm, corner_hbm, wqkv_hbm, wout_hbm, pack_hbm, packt_hbm, spread_hbm,
    spreadt_hbm,
    mixed_hbm, gin_hbm,
    x_v, do_v, gain_v, corner_v, w_v, wo_v, pack_v, packt_v, spread_v, spreadt_v,
    xn_v, xh_v, inv_v, q_v, da_v, kvx_v, kt_v, mask_v, dk_v, dv_v,
    att_v, g_v, gh_v, dn_v, mixed_v, gin_v,
    edge1_v, rim1_r, edge1_r, send2_v, recv2_v,
    in_sem, w_sem, out_sem, send1_sem, recv1_sem, send2_sem, recv2_sem,
):
    f32, bf16 = jnp.float32, jnp.bfloat16
    lon, lev = lax.axis_index("lon"), lax.axis_index("lev")
    lons, levs = lax.axis_size("lon"), lax.axis_size("lev")
    target = [
        {"lon": lax.rem(lon + dx + lons, lons), "lev": lax.rem(lev + dy + levs, levs)}
        for dy, dx in AROUND
    ]

    small = [
        pltpu.make_async_copy(src, dst, in_sem.at[i])
        for i, (src, dst) in enumerate(
            [
                (x_hbm, x_v), (pack_hbm, pack_v), (corner_hbm, corner_v), (gain_hbm, gain_v),
                (do_hbm, do_v), (spread_hbm, spread_v), (spreadt_hbm, spreadt_v),
                (packt_hbm, packt_v),
            ]
        )
    ]
    for copy in small:
        copy.start()

    def weight(c):
        return pltpu.make_async_copy(wqkv_hbm.at[:, lanes(c)], w_v.at[:, lanes(c)], w_sem.at[c])

    out_weight = pltpu.make_async_copy(wout_hbm, wo_v, w_sem.at[3 * QUADS])
    for c in range(3 * QUADS):
        weight(c).start()
    out_weight.start()

    barrier = pltpu.get_barrier_semaphore()
    for device in target:
        pl.semaphore_signal(
            barrier, inc=1, device_id=device, device_id_type=pl.DeviceIdType.MESH
        )

    def remote(src, dst, d, send_sem, recv_sem):
        return pltpu.make_async_remote_copy(
            src_ref=src,
            dst_ref=dst,
            send_sem=send_sem.at[d],
            recv_sem=recv_sem.at[OPPOSITE[d]],
            device_id=target[d],
            device_id_type=pl.DeviceIdType.MESH,
        )

    small[0].wait()
    small[1].wait()
    edge1_v[...] = dot(pack_v[...], x_v[...]).astype(bf16)
    pl.semaphore_wait(barrier, len(target))
    first = [
        remote(x_hbm.at[pl.ds(0, RIM)], rim1_r.at[pl.ds(RIM, RIM)], 0, send1_sem, recv1_sem),
        remote(x_hbm.at[pl.ds(CELLS - RIM, RIM)], rim1_r.at[pl.ds(0, RIM)], 1, send1_sem, recv1_sem),
    ]
    for i, (_, at, size) in enumerate(PIECES):
        other = PIECES[OPPOSITE[2 + i] - 2][1]
        first.append(
            remote(
                edge1_v.at[pl.ds(at, size)], edge1_r.at[pl.ds(other, size)], 2 + i,
                send1_sem, recv1_sem,
            )
        )
    for copy in first:
        copy.start()

    small[2].wait()
    codes = corner_v[...].astype(f32).astype(bf16)
    key_at = lax.broadcasted_iota(jnp.int32, (SPAN, QUAD), 0)
    query_at = lax.broadcasted_iota(jnp.int32, (SPAN, QUAD), 1)
    ext_row, position = key_at >> 4, key_at & 15
    query_row, query_col = (query_at >> 3) & 7, query_at & 7
    key_col = jnp.where(position >= 13, position - 16, position)
    near_row = ext_row - RADIUS - query_row
    near_col = key_col - query_col
    key_row = lev * ROWS + ext_row - RADIUS
    fine = (
        (jnp.abs(near_row) <= RADIUS)
        & (jnp.abs(near_col) <= RADIUS)
        & ((position < 11) | (position > 12))
        & (key_row >= 0)
        & (key_row < levs * ROWS)
    )
    leaves = jnp.where(
        (near_row == 0) | (near_col == 0),
        -1,
        1 + jnp.where(near_row > 0, 2, 0) + jnp.where(near_col > 0, 1, 0),
    ).astype(f32)
    leaves = jnp.where(fine, leaves, -2.0)
    pick_col = lax.broadcasted_iota(jnp.int32, (COLS, QUAD), 0)
    pick_lane = lax.broadcasted_iota(jnp.int32, (COLS, QUAD), 1)
    row_of = lax.broadcasted_iota(jnp.int32, (ROWS, QUAD), 0)
    lane_row = (lax.broadcasted_iota(jnp.int32, (ROWS, QUAD), 1) >> 3) & 7
    for t in range(TILES):
        pick = jnp.where(pick_col == t * TILE + (pick_lane & 7), 1.0, 0.0).astype(bf16)
        spread_codes = dot(codes, pick)
        code = jnp.sum(
            jnp.where(row_of == lane_row, spread_codes, 0.0), axis=0, keepdims=True
        )
        mask_v[t] = jnp.where((leaves == code) | (leaves < -1.5), NEG, 0.0)

    small[3].wait()
    gain = gain_v[...]

    def normed(x):
        inv = lax.rsqrt(jnp.mean(x * x, axis=-1, keepdims=True) + EPSILON)
        return inv, (x * inv * gain).astype(bf16)

    inv_own, own = normed(x_v[...].astype(f32))
    xn_v[...] = own
    inv_v[...] = jnp.broadcast_to(inv_own, (CELLS, 128))

    def by_tiles(y):
        y = y.reshape(ROWS, TILES, TILE, QUAD)
        return jnp.concatenate([y[:, t] for t in range(TILES)], axis=0).reshape(CELLS, QUAD)

    @pl.loop(0, QUADS)
    def _(c):
        weight(c).wait()
        y = dot(xn_v[...], w_v[:, lanes(c)]) * (HEAD_DIM**-0.5)
        q_v[:, lanes(c)] = by_tiles(y).astype(bf16)

    @pl.loop(0, 2 * QUADS)
    def _(c):
        weight(QUADS + c).wait()
        y = dot(xn_v[...], w_v[:, lanes(QUADS + c)])
        kvx_v[pl.ds(RADIUS, ROWS), pl.ds(0, COLS), lanes(c)] = y.reshape(ROWS, COLS, QUAD)

    small[4].wait()
    out_weight.wait()

    @pl.loop(0, QUADS)
    def _(c):
        y = dot(do_v[...], wo_v[lanes(c), :], ROWS_BY_ROWS)
        da_v[:, lanes(c)] = by_tiles(y).astype(bf16)

    small[5].wait()
    small[6].wait()
    for copy in first:
        copy.wait_recv()
    xh_v[pl.ds(0, 2 * RIM)] = normed(rim1_r[...].astype(f32))[1]
    xh_v[pl.ds(2 * RIM, EDGE)] = normed(dot(spread_v[...], edge1_r[...]))[1]

    low_side = lax.broadcasted_iota(jnp.int32, (EXT, TILE, QUAD), 1) < 4

    @pl.loop(0, 2 * QUADS)
    def _(c):
        y = dot(xh_v[...], w_v[:, lanes(QUADS + c)])
        kvx_v[pl.ds(0, RADIUS), pl.ds(0, COLS), lanes(c)] = y[:RIM].reshape(RADIUS, COLS, QUAD)
        kvx_v[pl.ds(RADIUS + ROWS, RADIUS), pl.ds(0, COLS), lanes(c)] = y[RIM : 2 * RIM].reshape(
            RADIUS, COLS, QUAD
        )
        edge = y[2 * RIM :].reshape(EXT, TILE, QUAD)
        for t in range(TILES):
            main = kvx_v[:, pl.ds(t * TILE, TILE), lanes(c)]
            east = edge if t == TILES - 1 else kvx_v[:, pl.ds((t + 1) * TILE, TILE), lanes(c)]
            west = edge if t == 0 else kvx_v[:, pl.ds((t - 1) * TILE, TILE), lanes(c)]
            side = jnp.where(low_side, east, west)
            kt_v[t, :, lanes(c)] = (
                jnp.concatenate([main, side], axis=1).reshape(SPAN, QUAD).astype(bf16)
            )

    lane_head = lax.broadcasted_iota(jnp.int32, (TILE * ROWS, QUAD), 1) >> 6
    head_masks = [jnp.where(lane_head == h, 1.0, 0.0).astype(bf16) for h in range(4)]

    def stacked(y):
        return jnp.concatenate([y * mask for mask in head_masks], axis=0)

    def unstacked(y):
        n = TILE * ROWS
        out = y[:n]
        for h in range(1, 4):
            out = jnp.where(lane_head == h, y[h * n : (h + 1) * n], out)
        return out

    @pl.loop(0, QUADS)
    def _(j):
        atts, gqs = [], []
        for t in range(TILES):
            key, value = kt_v[t, :, lanes(j)], kt_v[t, :, lanes(QUADS + j)]
            cells = pl.ds(t * TILE * ROWS, TILE * ROWS)
            query, d_attn = stacked(q_v[cells, lanes(j)]), stacked(da_v[cells, lanes(j)])
            terms = jnp.exp(dot(key, query, ROWS_BY_ROWS) + mask_v[t])
            weights = terms * (1.0 / jnp.sum(terms, axis=0, keepdims=True))
            weights_b = weights.astype(bf16)
            grad_prob = dot(value, d_attn, ROWS_BY_ROWS)
            delta = jnp.sum(weights * grad_prob, axis=0, keepdims=True)
            dscore = (weights * (grad_prob - delta)).astype(bf16)
            atts.append(unstacked(dot(weights_b, value, COLS_BY_COLS)))
            gqs.append(unstacked(dot(dscore, key, COLS_BY_COLS)) * (HEAD_DIM**-0.5))
            dk_v[t] = dot(dscore, query).reshape(EXT, 2 * TILE, QUAD)
            dv_v[t] = dot(weights_b, d_attn).reshape(EXT, 2 * TILE, QUAD)

        def in_rows(parts):
            parts = [p.reshape(ROWS, TILE, QUAD) for p in parts]
            return jnp.concatenate(parts, axis=1).reshape(CELLS, QUAD).astype(bf16)

        att_v[:, lanes(j)] = in_rows(atts)
        g_v[:, lanes(j)] = in_rows(gqs)
        for d_ref, block in ((dk_v, j), (dv_v, QUADS + j)):
            sides = [d_ref[t, :, pl.ds(TILE, TILE), :] for t in range(TILES)]
            groups = []
            for t in range(TILES):
                low = sides[t - 1] if t > 0 else 0.0
                high = sides[t + 1] if t < TILES - 1 else 0.0
                groups.append(d_ref[t, :, pl.ds(0, TILE), :] + jnp.where(low_side, low, high))
            whole = jnp.concatenate(groups, axis=1)
            g_v[:, lanes(QUADS + block)] = (
                whole[RADIUS : RADIUS + ROWS].reshape(CELLS, QUAD).astype(bf16)
            )
            gh_v[pl.ds(0, RIM), lanes(block)] = whole[:RADIUS].reshape(RIM, QUAD).astype(bf16)
            gh_v[pl.ds(RIM, RIM), lanes(block)] = (
                whole[RADIUS + ROWS :].reshape(RIM, QUAD).astype(bf16)
            )
            edge = jnp.where(low_side, sides[-1], sides[0]).reshape(EDGE, QUAD).astype(bf16)
            gh_v[pl.ds(2 * RIM, PACK), lanes(block)] = dot(spreadt_v[...], edge).astype(bf16)

    @pl.loop(0, QUADS)
    def _(n):
        y = dot(gh_v[...], w_v[lanes(n), pl.ds(WIDTH, 2 * WIDTH)], ROWS_BY_ROWS)
        send2_v[:, lanes(n)] = y.astype(bf16)

    second = [
        remote(send2_v.at[pl.ds(0, RIM)], recv2_v.at[pl.ds(RIM, RIM)], 0, send2_sem, recv2_sem),
        remote(send2_v.at[pl.ds(RIM, RIM)], recv2_v.at[pl.ds(0, RIM)], 1, send2_sem, recv2_sem),
    ]
    for i, (_, at, size) in enumerate(PIECES):
        other = PIECES[OPPOSITE[2 + i] - 2][1]
        second.append(
            remote(
                send2_v.at[pl.ds(2 * RIM + at, size)], recv2_v.at[pl.ds(2 * RIM + other, size)],
                2 + i, send2_sem, recv2_sem,
            )
        )
    for copy in second:
        copy.start()

    @pl.loop(0, QUADS)
    def _(n):
        mixed_v[:, lanes(n)] = dot(att_v[...], wo_v[:, lanes(n)]).astype(bf16)

    mixed_copy = pltpu.make_async_copy(mixed_v, mixed_hbm, out_sem.at[0])
    mixed_copy.start()

    @pl.loop(0, QUADS)
    def _(n):
        dn_v[:, lanes(n)] = dot(g_v[...], w_v[lanes(n), :], ROWS_BY_ROWS)

    small[7].wait()
    for copy in second:
        copy.wait_recv()
    dn_v[pl.ds(0, RIM)] += recv2_v[pl.ds(0, RIM)].astype(f32)
    dn_v[pl.ds(CELLS - RIM, RIM)] += recv2_v[pl.ds(RIM, RIM)].astype(f32)
    scaled = (dn_v[...] + dot(packt_v[...], recv2_v[pl.ds(2 * RIM, PACK)])) * gain
    x = x_v[...].astype(f32)
    inv = inv_v[:, :1]
    mean = jnp.mean(x * scaled, axis=-1, keepdims=True)
    gin_v[...] = (inv * scaled - x * (inv * inv * inv * mean)).astype(bf16)
    gin_copy = pltpu.make_async_copy(gin_v, gin_hbm, out_sem.at[1])
    gin_copy.start()
    mixed_copy.wait()
    gin_copy.wait()
    for copy in first + second:
        copy.wait_send()


def shards(inputs, norm_gain, w_qkv, w_out, d_out, corner):
    assert inputs.shape == (ROWS, COLS, WIDTH), inputs.shape
    f32, bf16 = jnp.float32, jnp.bfloat16
    pack, spread = selections()
    vmem, dma = pltpu.VMEM, pltpu.SemaphoreType.DMA
    anywhere = pl.BlockSpec(memory_space=pl.ANY)
    mixed_out, grad_input = pl.pallas_call(
        kernel,
        out_shape=[jax.ShapeDtypeStruct((CELLS, WIDTH), bf16)] * 2,
        in_specs=[anywhere] * 10,
        out_specs=[anywhere] * 2,
        scratch_shapes=[
            vmem((CELLS, WIDTH), bf16),
            vmem((CELLS, WIDTH), bf16),
            vmem((1, WIDTH), f32),
            vmem((ROWS, COLS), jnp.int32),
            vmem((WIDTH, 3 * WIDTH), bf16),
            vmem((WIDTH, WIDTH), bf16),
            vmem((PACK, CELLS), bf16),
            vmem((CELLS, PACK), bf16),
            vmem((EDGE, PACK), bf16),
            vmem((PACK, EDGE), bf16),
            vmem((CELLS, WIDTH), bf16),
            vmem((2 * RIM + EDGE, WIDTH), bf16),
            vmem((CELLS, 128), f32),
            vmem((CELLS, WIDTH), bf16),
            vmem((CELLS, WIDTH), bf16),
            vmem((EXT, COLS, 2 * WIDTH), f32),
            vmem((TILES, SPAN, 2 * WIDTH), bf16),
            vmem((TILES, SPAN, QUAD), f32),
            vmem((TILES, EXT, 2 * TILE, QUAD), f32),
            vmem((TILES, EXT, 2 * TILE, QUAD), f32),
            vmem((CELLS, WIDTH), bf16),
            vmem((CELLS, 3 * WIDTH), bf16),
            vmem((HALO, 2 * WIDTH), bf16),
            vmem((CELLS, WIDTH), f32),
            vmem((CELLS, WIDTH), bf16),
            vmem((CELLS, WIDTH), bf16),
            vmem((PACK, WIDTH), bf16),
            vmem((2 * RIM, WIDTH), bf16),
            vmem((PACK, WIDTH), bf16),
            vmem((HALO, WIDTH), bf16),
            vmem((HALO, WIDTH), bf16),
            dma((8,)),
            dma((3 * QUADS + 1,)),
            dma((2,)),
            dma((8,)),
            dma((8,)),
            dma((8,)),
            dma((8,)),
        ],
        compiler_params=pltpu.CompilerParams(
            collective_id=0, has_side_effects=True, vmem_limit_bytes=56 * 1024 * 1024
        ),
    )(
        inputs.reshape(CELLS, WIDTH),
        d_out.reshape(CELLS, WIDTH),
        norm_gain.reshape(1, WIDTH),
        corner,
        w_qkv,
        w_out,
        jnp.asarray(pack, bf16),
        jnp.asarray(pack.T, bf16),
        jnp.asarray(spread, bf16),
        jnp.asarray(spread.T, bf16),
    )
    return mixed_out.reshape(inputs.shape), grad_input.reshape(inputs.shape)


def solution(mesh):
    placed = (P("lev", "lon", None), P(), P(), P(), P("lev", "lon", None), P("lev", "lon"))
    return jax.shard_map(
        shards,
        mesh=mesh,
        in_specs=placed,
        out_specs=(P("lev", "lon", None), P("lev", "lon", None)),
        check_vma=False,
    )
```

```python
import jax
import jax.numpy as jnp
from jax import lax
from jax.experimental import pallas as pl
from jax.experimental.pallas import tpu as pltpu
from jax.sharding import PartitionSpec as P

HEADS = 16
RADIUS = 3
EPSILON = 1e-06

ROWS, COLS, WIDTH = 8, 32, 1024
CELLS = ROWS * COLS
HEAD_DIM = WIDTH // HEADS
QUAD = 4 * HEAD_DIM
QUADS = WIDTH // QUAD
TILE = 8
TILES = COLS // TILE
EXT = ROWS + 2 * RADIUS
SPAN = EXT * 2 * TILE
HALF = COLS // 2
RIM = RADIUS * HALF
SIDE = 64
EDGE = EXT * TILE
PACK = 128
PART = 2 * RIM + EDGE
LATE = 2 * RIM + PACK
NEG = -1e30

PIECES = (
    ((0, -1), 0, 32),
    ((-1, -1), 32, 16),
    ((1, -1), 48, 16),
    ((0, 1), 64, 32),
    ((-1, 1), 96, 16),
    ((1, 1), 112, 16),
)
AROUND = ((-1, 0), (1, 0)) + tuple(p[0] for p in PIECES)
OPPOSITE = tuple(AROUND.index((-d[0], -d[1])) for d in AROUND)


def piece_places(p):
    east, r = p >> 6, p & 63
    north, south = (r >= 32) & (r < 48), r >= 48
    i = jnp.where(south, r - 48, jnp.where(north, r - 32, r))
    row = (i * 43) >> 7
    c = i - 3 * row
    valid = row < jnp.where(north | south, RADIUS, ROWS)
    own_row = row + jnp.where(south, ROWS - RADIUS, 0)
    ext_row = row + jnp.where(south, RADIUS + ROWS, jnp.where(north, 0, RADIUS))
    cell = own_row * COLS + c + (COLS - RADIUS) * east
    edge = ext_row * TILE + c + (TILE - RADIUS) * (1 - east)
    return jnp.where(valid, cell, -1), jnp.where(valid, edge, -1)


def selection(shape, axis, which, first=0):
    p = lax.broadcasted_iota(jnp.int32, shape, axis) + first
    other = lax.broadcasted_iota(jnp.int32, shape, 1 - axis)
    return jnp.where(piece_places(p)[which] == other, 1.0, 0.0).astype(jnp.bfloat16)


def dot(a, b, dims=((1,), (0,))):
    return lax.dot_general(a, b, (dims, ((), ())), preferred_element_type=jnp.float32)


ROWS_BY_ROWS = ((1,), (1,))
COLS_BY_COLS = ((0,), (0,))


def lanes(index, size=QUAD):
    if isinstance(index, int):
        return pl.ds(index * size, size)
    return pl.ds(pl.multiple_of(index * size, size), size)


def kernel(
    x_hbm, do_hbm, gain_hbm, corner_hbm, wqkv_hbm, wout_hbm,
    mixed_o, scaled_o, inv_o,
    x_v, do_v, gain_v, corner_v, w_v, wo_v, pack_v, packt_v, west_v, east_v, spreadt_v,
    xn_v, xh_v, q_v, da_v, kvx_v, kt_v, mask_v, dk_v, dv_v,
    attf_v, gqf_v, att_v, g_v, gh1_v, gh2_v,
    edge1_v, rim1_r, edge1_r, send2a_v, recv2a_r, send2b_v, recv2b_r,
    in_sem, w_sem, send1_sem, recv1_sem, send2_sem, recv2_sem,
):
    f32, bf16 = jnp.float32, jnp.bfloat16
    lon, lev = lax.axis_index("lon"), lax.axis_index("lev")
    lons, levs = lax.axis_size("lon"), lax.axis_size("lev")
    target = [
        {"lon": lax.rem(lon + dx + lons, lons), "lev": lax.rem(lev + dy + levs, levs)}
        for dy, dx in AROUND
    ]
    barrier = pltpu.get_barrier_semaphore()
    for device in target:
        pl.semaphore_signal(
            barrier, inc=1, device_id=device, device_id_type=pl.DeviceIdType.MESH
        )

    small = [
        pltpu.make_async_copy(src, dst, in_sem.at[i])
        for i, (src, dst) in enumerate(
            [
                (x_hbm, x_v), (corner_hbm, corner_v), (gain_hbm, gain_v), (do_hbm, do_v),
            ]
        )
    ]
    for copy in small[:3]:
        copy.start()
    pack_v[...] = selection((PACK, CELLS), 0, 0)

    def weight(c):
        return pltpu.make_async_copy(wqkv_hbm.at[:, lanes(c)], w_v.at[:, lanes(c)], w_sem.at[c])

    out_weight = pltpu.make_async_copy(wout_hbm, wo_v, w_sem.at[3 * QUADS])

    def remote(src, dst, d, slot, send_sem, recv_sem):
        return pltpu.make_async_remote_copy(
            src_ref=src,
            dst_ref=dst,
            send_sem=send_sem.at[slot],
            recv_sem=recv_sem.at[slot],
            device_id=target[d],
            device_id_type=pl.DeviceIdType.MESH,
        )

    def rims(src, dst, slot, send_sem, recv_sem):
        return [
            remote(src[0], dst[1], 0, slot, send_sem, recv_sem),
            remote(src[1], dst[0], 1, slot + 1, send_sem, recv_sem),
        ]

    def pieces(src, dst, base, indices, slot, send_sem, recv_sem):
        copies = []
        for n, i in enumerate(indices):
            at, size = PIECES[i][1:]
            other = PIECES[OPPOSITE[2 + i] - 2][1]
            copies.append(
                remote(
                    src.at[pl.ds(base + at, size)], dst.at[pl.ds(base + other, size)], 2 + i,
                    slot + n, send_sem, recv_sem,
                )
            )
        return copies

    def halves(ref, half):
        columns = pl.ds(half * HALF, HALF)
        return [ref.at[pl.ds(0, RADIUS), columns], ref.at[pl.ds(ROWS - RADIUS, RADIUS), columns]]

    def arrivals(half):
        columns = pl.ds(half * HALF, HALF)
        return [rim1_r.at[pl.ds(0, RADIUS), columns], rim1_r.at[pl.ds(RADIUS, RADIUS), columns]]

    first = [
        rims(halves(x_hbm, p), arrivals(p), 5 * p, send1_sem, recv1_sem)
        + pieces(
            edge1_v, edge1_r, 0, (3, 4, 5) if p == 0 else (0, 1, 2), 5 * p + 2, send1_sem,
            recv1_sem,
        )
        for p in range(2)
    ]
    pl.semaphore_wait(barrier, len(target))
    for copy in first[0][:2]:
        copy.start()
    small[0].wait()
    x_own = x_v[...].reshape(CELLS, WIDTH)
    edge1_v[...] = dot(pack_v[...], x_own).astype(bf16)
    for copy in first[0][2:]:
        copy.start()
    for c in range(3 * QUADS):
        weight(c).start()
    small[3].start()
    out_weight.start()
    packt_v[...] = selection((CELLS, PACK), 1, 0)
    west_v[...] = selection((EDGE, SIDE), 1, 1)
    east_v[...] = selection((EDGE, SIDE), 1, 1, SIDE)
    spreadt_v[...] = selection((PACK, EDGE), 0, 1)

    small[1].wait()
    codes = corner_v[...].astype(f32).astype(bf16)
    key_at = lax.broadcasted_iota(jnp.int32, (SPAN, 128), 0)
    query_at = lax.broadcasted_iota(jnp.int32, (SPAN, 128), 1)
    ext_row, position = key_at >> 4, key_at & 15
    query_row, query_col = (query_at >> 3) & 7, query_at & 7
    key_col = jnp.where(position >= 13, position - 16, position)
    near_row = ext_row - RADIUS - query_row
    near_col = key_col - query_col
    key_row = lev * ROWS + ext_row - RADIUS
    fine = (
        (jnp.abs(near_row) <= RADIUS)
        & (jnp.abs(near_col) <= RADIUS)
        & ((position < 11) | (position > 12))
        & (key_row >= 0)
        & (key_row < levs * ROWS)
    )
    leaves = jnp.where(
        (near_row == 0) | (near_col == 0),
        -1,
        1 + jnp.where(near_row > 0, 2, 0) + jnp.where(near_col > 0, 1, 0),
    ).astype(f32)
    leaves = jnp.where(fine, leaves, -2.0)
    pick_col = lax.broadcasted_iota(jnp.int32, (COLS, 128), 0)
    pick_lane = lax.broadcasted_iota(jnp.int32, (COLS, 128), 1)
    row_of = lax.broadcasted_iota(jnp.int32, (ROWS, 128), 0)
    lane_row = (lax.broadcasted_iota(jnp.int32, (ROWS, 128), 1) >> 3) & 7
    for t in range(TILES):
        pick = jnp.where(pick_col == t * TILE + (pick_lane & 7), 1.0, 0.0).astype(bf16)
        spread_codes = dot(codes, pick)
        code = jnp.sum(
            jnp.where(row_of == lane_row, spread_codes, 0.0), axis=0, keepdims=True
        )
        mask_v[t] = jnp.where((leaves == code) | (leaves < -1.5), NEG, 0.0)

    small[2].wait()
    gain = gain_v[...]

    def normed(x):
        inv = lax.rsqrt(jnp.mean(x * x, axis=-1, keepdims=True) + EPSILON)
        return inv, (x * inv * gain).astype(bf16)

    inv_own, own = normed(x_own.astype(f32))
    xn_v[...] = own
    inv_o[...] = jnp.broadcast_to(inv_own, (CELLS, 128))

    def by_tiles(y):
        y = y.reshape(ROWS, TILES, TILE, QUAD)
        return jnp.concatenate([y[:, t] for t in range(TILES)], axis=0).reshape(CELLS, QUAD)

    @pl.loop(0, QUADS)
    def _(c):
        weight(c).wait()
        y = dot(xn_v[...], w_v[:, lanes(c)]) * (HEAD_DIM**-0.5)
        q_v[:, lanes(c)] = by_tiles(y).astype(bf16)

    for copy in first[1]:
        copy.start()

    @pl.loop(0, 2 * QUADS)
    def _(c):
        weight(QUADS + c).wait()
        y = dot(xn_v[...], w_v[:, lanes(QUADS + c)])
        kvx_v[pl.ds(RADIUS, ROWS), pl.ds(0, COLS), lanes(c)] = y.reshape(ROWS, COLS, QUAD)

    small[3].wait()
    out_weight.wait()

    @pl.loop(0, QUADS)
    def _(c):
        y = dot(do_v[...], wo_v[lanes(c), :], ROWS_BY_ROWS)
        da_v[:, lanes(c)] = by_tiles(y).astype(bf16)

    low_side = lax.broadcasted_iota(jnp.int32, (EXT, TILE, QUAD), 1) < 4

    def received(p, tiles):
        for copy in first[p]:
            copy.wait_recv()
        rim = rim1_r[:, pl.ds(p * HALF, HALF)].reshape(2 * RIM, WIDTH)
        xh_v[pl.ds(0, 2 * RIM)] = normed(rim.astype(f32))[1]
        edge = dot((east_v if p else west_v)[...], edge1_r[pl.ds(p * SIDE, SIDE)])
        xh_v[pl.ds(2 * RIM, EDGE)] = normed(edge)[1]

        @pl.loop(0, 2 * QUADS, unroll=4)
        def _(c):
            y = dot(xh_v[...], w_v[:, lanes(QUADS + c)])
            rim = y[: 2 * RIM].reshape(2, RADIUS, HALF, QUAD)
            kvx_v[pl.ds(0, RADIUS), pl.ds(p * HALF, HALF), lanes(c)] = rim[0]
            kvx_v[pl.ds(RADIUS + ROWS, RADIUS), pl.ds(p * HALF, HALF), lanes(c)] = rim[1]
            kvx_v[:, pl.ds(COLS + p * TILE, TILE), lanes(c)] = y[2 * RIM :].reshape(
                EXT, TILE, QUAD
            )
            for t in tiles:
                main = kvx_v[:, pl.ds(t * TILE, TILE), lanes(c)]
                east = kvx_v[:, pl.ds((t + 1 if t < TILES - 1 else TILES + 1) * TILE, TILE), lanes(c)]
                west = kvx_v[:, pl.ds((t - 1 if t > 0 else TILES) * TILE, TILE), lanes(c)]
                side = jnp.where(low_side, east, west)
                kt_v[t, :, lanes(c)] = (
                    jnp.concatenate([main, side], axis=1).reshape(SPAN, QUAD).astype(bf16)
                )

    lane_head = lax.broadcasted_iota(jnp.int32, (TILE * ROWS, QUAD), 1) >> 6
    head_masks = [jnp.where(lane_head == h, 1.0, 0.0).astype(bf16) for h in range(4)]

    def stacked(y):
        return jnp.concatenate([y * mask for mask in head_masks], axis=0)

    def unstacked(y):
        n = TILE * ROWS
        out = y[:n]
        for h in range(1, 4):
            out = jnp.where(lane_head == h, y[h * n : (h + 1) * n], out)
        return out.reshape(ROWS, TILE, QUAD)

    def attend(t, j):
        key, value = kt_v[t, :, lanes(j)], kt_v[t, :, lanes(QUADS + j)]
        cells, columns = pl.ds(t * TILE * ROWS, TILE * ROWS), pl.ds(t * TILE, TILE)
        query, d_attn = stacked(q_v[cells, lanes(j)]), stacked(da_v[cells, lanes(j)])
        scores = dot(key, query, ROWS_BY_ROWS)
        grad_probs = dot(value, d_attn, ROWS_BY_ROWS)
        mask = mask_v[t]
        weights_b, dscore = [], []
        for half in range(2):
            part = slice(half * 128, (half + 1) * 128)
            terms = jnp.exp(scores[:, part] + mask)
            weights = terms * (1.0 / jnp.sum(terms, axis=0, keepdims=True))
            weights_b.append(weights.astype(bf16))
            grad_prob = grad_probs[:, part]
            delta = jnp.sum(weights * grad_prob, axis=0, keepdims=True)
            dscore.append((weights * (grad_prob - delta)).astype(bf16))
        weights_b, dscore = (jnp.concatenate(y, axis=1) for y in (weights_b, dscore))
        attf_v[:, columns, lanes(j)] = unstacked(dot(weights_b, value, COLS_BY_COLS))
        gqf_v[:, columns, lanes(j)] = unstacked(dot(dscore, key, COLS_BY_COLS)) * (
            HEAD_DIM**-0.5
        )
        dk_v[t, :, :, lanes(j)] = dot(dscore, query).reshape(EXT, 2 * TILE, QUAD)
        dv_v[t, :, :, lanes(j)] = dot(weights_b, d_attn).reshape(EXT, 2 * TILE, QUAD)

    def gathered(j, half, gh_ref):
        for d_ref, block in ((dk_v, j), (dv_v, QUADS + j)):
            groups = []
            for t in (2 * half, 2 * half + 1):
                low = d_ref[t - 1, :, pl.ds(TILE, TILE), lanes(j)] if t > 0 else 0.0
                high = d_ref[t + 1, :, pl.ds(TILE, TILE), lanes(j)] if t < TILES - 1 else 0.0
                main = d_ref[t, :, pl.ds(0, TILE), lanes(j)]
                groups.append(main + jnp.where(low_side, low, high))
            whole = jnp.concatenate(groups, axis=1).astype(bf16)
            g_v[:, pl.ds(half * HALF, HALF), lanes(QUADS + block)] = whole[
                RADIUS : RADIUS + ROWS
            ]
            gh_ref[pl.ds(0, RIM), lanes(block)] = whole[:RADIUS].reshape(RIM, QUAD)
            gh_ref[pl.ds(RIM, RIM), lanes(block)] = whole[RADIUS + ROWS :].reshape(RIM, QUAD)
            if half == 1:
                east = d_ref[TILES - 1, :, pl.ds(TILE, TILE), lanes(j)]
                west = d_ref[0, :, pl.ds(TILE, TILE), lanes(j)]
                edge = jnp.where(low_side, east, west).reshape(EDGE, QUAD).astype(bf16)
                gh_ref[pl.ds(2 * RIM, PACK), lanes(block)] = dot(spreadt_v[...], edge).astype(bf16)

    def projected(gh_ref, out_ref):
        @pl.loop(0, QUADS, unroll=True)
        def _(n):
            y = dot(gh_ref[...], w_v[lanes(n), pl.ds(WIDTH, 2 * WIDTH)], ROWS_BY_ROWS)
            out_ref[:, lanes(n)] = y.astype(bf16)

    received(0, (0,))

    @pl.loop(0, QUADS // 2)
    def _(j):
        attend(0, 2 * j)
        attend(0, 2 * j + 1)

    received(1, (1, 2, 3))

    @pl.loop(0, QUADS)
    def _(j):
        attend(1, j)
        attend(2, j)
        gathered(j, 0, gh1_v)

    projected(gh1_v, send2a_v)
    n_s = [pl.ds(0, RIM), pl.ds(RIM, RIM)]
    second = rims(
        [send2a_v.at[d] for d in n_s], [recv2a_r.at[d] for d in n_s], 0, send2_sem, recv2_sem
    )
    for copy in second:
        copy.start()

    @pl.loop(0, QUADS // 2)
    def _(j):
        for k in range(2):
            attend(3, 2 * j + k)
            gathered(2 * j + k, 1, gh2_v)

    projected(gh2_v, send2b_v)
    third = rims(
        [send2b_v.at[d] for d in n_s], [recv2b_r.at[d] for d in n_s], 2, send2_sem, recv2_sem
    ) + pieces(send2b_v, recv2b_r, 2 * RIM, range(6), 4, send2_sem, recv2_sem)
    for copy in third:
        copy.start()

    att_v[...] = attf_v[...].astype(bf16).reshape(CELLS, WIDTH)
    g_v[:, :, pl.ds(0, WIDTH)] = gqf_v[...].astype(bf16)

    @pl.loop(0, QUADS)
    def _(n):
        mixed_o[:, lanes(n)] = dot(att_v[...], wo_v[:, lanes(n)]).astype(bf16)

    @pl.loop(0, QUADS)
    def _(n):
        scaled_o[:, lanes(n)] = dot(
            g_v[...].reshape(CELLS, 3 * WIDTH), w_v[lanes(n), :], ROWS_BY_ROWS
        )

    for copy in second + third:
        copy.wait_recv()

    def both(rows):
        west, east = (r[rows].astype(f32).reshape(RADIUS, HALF, WIDTH) for r in (recv2a_r, recv2b_r))
        return jnp.concatenate([west, east], axis=1).reshape(2 * RIM, WIDTH)

    scaled_o[pl.ds(0, 2 * RIM)] += both(n_s[0])
    scaled_o[pl.ds(CELLS - 2 * RIM, 2 * RIM)] += both(n_s[1])
    edges = dot(packt_v[...], recv2b_r[pl.ds(2 * RIM, PACK)])
    scaled_o[...] = (scaled_o[...] + edges) * gain
    for copy in first[0] + first[1] + second + third:
        copy.wait_send()


def finish(x_ref, mixed_ref, scaled_ref, inv_ref, mixed_hbm, gin_hbm, gin_v, sem):
    mixed_copy = pltpu.make_async_copy(mixed_ref, mixed_hbm, sem.at[0])
    mixed_copy.start()
    blocks = 4
    size = CELLS // blocks
    copies = []
    for b in range(blocks):
        rows = pl.ds(b * size, size)
        x, scaled, inv = x_ref[rows].astype(jnp.float32), scaled_ref[rows], inv_ref[rows][:, :1]
        mean = jnp.mean(x * scaled, axis=-1, keepdims=True)
        gin_v[rows] = (inv * scaled - x * (inv * inv * inv * mean)).astype(gin_v.dtype)
        copies.append(pltpu.make_async_copy(gin_v.at[rows], gin_hbm.at[rows], sem.at[1 + b]))
        copies[-1].start()
    for copy in [mixed_copy] + copies:
        copy.wait()


def shards(inputs, norm_gain, w_qkv, w_out, d_out, corner):
    assert inputs.shape == (ROWS, COLS, WIDTH), inputs.shape
    f32, bf16 = jnp.float32, jnp.bfloat16
    vmem, dma = pltpu.VMEM, pltpu.SemaphoreType.DMA
    anywhere = pl.BlockSpec(memory_space=pl.ANY)
    inside = pl.BlockSpec(memory_space=pltpu.VMEM)
    mixed, scaled, inv = pl.pallas_call(
        kernel,
        out_shape=[
            vmem((CELLS, WIDTH), bf16),
            vmem((CELLS, WIDTH), f32),
            vmem((CELLS, 128), f32),
        ],
        in_specs=[anywhere] * 6,
        out_specs=[inside] * 3,
        scratch_shapes=[
            vmem((ROWS, COLS, WIDTH), bf16),
            vmem((CELLS, WIDTH), bf16),
            vmem((1, WIDTH), f32),
            vmem((ROWS, COLS), jnp.int32),
            vmem((WIDTH, 3 * WIDTH), bf16),
            vmem((WIDTH, WIDTH), bf16),
            vmem((PACK, CELLS), bf16),
            vmem((CELLS, PACK), bf16),
            vmem((EDGE, SIDE), bf16),
            vmem((EDGE, SIDE), bf16),
            vmem((PACK, EDGE), bf16),
            vmem((CELLS, WIDTH), bf16),
            vmem((PART, WIDTH), bf16),
            vmem((CELLS, WIDTH), bf16),
            vmem((CELLS, WIDTH), bf16),
            vmem((EXT, COLS + 2 * TILE, 2 * WIDTH), f32),
            vmem((TILES, SPAN, 2 * WIDTH), bf16),
            vmem((TILES, SPAN, 128), f32),
            vmem((TILES, EXT, 2 * TILE, WIDTH), f32),
            vmem((TILES, EXT, 2 * TILE, WIDTH), f32),
            vmem((ROWS, COLS, WIDTH), f32),
            vmem((ROWS, COLS, WIDTH), f32),
            vmem((CELLS, WIDTH), bf16),
            vmem((ROWS, COLS, 3 * WIDTH), bf16),
            vmem((2 * RIM, 2 * WIDTH), bf16),
            vmem((LATE, 2 * WIDTH), bf16),
            vmem((PACK, WIDTH), bf16),
            vmem((2 * RADIUS, COLS, WIDTH), bf16),
            vmem((PACK, WIDTH), bf16),
            vmem((2 * RIM, WIDTH), bf16),
            vmem((2 * RIM, WIDTH), bf16),
            vmem((LATE, WIDTH), bf16),
            vmem((LATE, WIDTH), bf16),
            dma((4,)),
            dma((3 * QUADS + 1,)),
            dma((10,)),
            dma((10,)),
            dma((10,)),
            dma((10,)),
        ],
        compiler_params=pltpu.CompilerParams(
            collective_id=0, has_side_effects=True, vmem_limit_bytes=61 * 1024 * 1024
        ),
    )(
        inputs,
        d_out.reshape(CELLS, WIDTH),
        norm_gain.reshape(1, WIDTH),
        corner,
        w_qkv,
        w_out,
    )
    mixed_out, grad_input = pl.pallas_call(
        finish,
        out_shape=[jax.ShapeDtypeStruct((CELLS, WIDTH), bf16)] * 2,
        in_specs=[inside] * 4,
        out_specs=[anywhere] * 2,
        scratch_shapes=[vmem((CELLS, WIDTH), bf16), dma((5,))],
        compiler_params=pltpu.CompilerParams(vmem_limit_bytes=16 * 1024 * 1024),
    )(inputs.reshape(CELLS, WIDTH), mixed, scaled, inv)
    return mixed_out.reshape(inputs.shape), grad_input.reshape(inputs.shape)


def solution(mesh):
    placed = (P("lev", "lon", None), P(), P(), P(), P("lev", "lon", None), P("lev", "lon"))
    return jax.shard_map(
        shards,
        mesh=mesh,
        in_specs=placed,
        out_specs=(P("lev", "lon", None), P("lev", "lon", None)),
        check_vma=False,
    )
```

```python
import jax
import jax.numpy as jnp
from jax import lax
from jax.experimental import pallas as pl
from jax.experimental.pallas import tpu as pltpu
from jax.sharding import PartitionSpec as P

HEADS = 16
RADIUS = 3
EPSILON = 1e-06

ROWS, COLS, WIDTH = 8, 32, 1024
CELLS = ROWS * COLS
HEAD_DIM = WIDTH // HEADS
QUAD = 4 * HEAD_DIM
QUADS = WIDTH // QUAD
TILE = 8
TILES = COLS // TILE
EXT = ROWS + 2 * RADIUS
SPAN = EXT * 2 * TILE
HALF = COLS // 2
RIM = RADIUS * HALF
SIDE = 64
EDGE = EXT * TILE
PACK = 128
PART = 2 * RIM + EDGE
LATE = 2 * RIM + PACK
NEG = -1e30

PIECES = (
    ((0, -1), 0, 32),
    ((-1, -1), 32, 16),
    ((1, -1), 48, 16),
    ((0, 1), 64, 32),
    ((-1, 1), 96, 16),
    ((1, 1), 112, 16),
)
AROUND = ((-1, 0), (1, 0)) + tuple(p[0] for p in PIECES)
OPPOSITE = tuple(AROUND.index((-d[0], -d[1])) for d in AROUND)


def piece_places(p):
    east, r = p >> 6, p & 63
    north, south = (r >= 32) & (r < 48), r >= 48
    i = jnp.where(south, r - 48, jnp.where(north, r - 32, r))
    row = (i * 43) >> 7
    c = i - 3 * row
    valid = row < jnp.where(north | south, RADIUS, ROWS)
    own_row = row + jnp.where(south, ROWS - RADIUS, 0)
    ext_row = row + jnp.where(south, RADIUS + ROWS, jnp.where(north, 0, RADIUS))
    cell = own_row * COLS + c + (COLS - RADIUS) * east
    edge = ext_row * TILE + c + (TILE - RADIUS) * (1 - east)
    return jnp.where(valid, cell, -1), jnp.where(valid, edge, -1)


def selection(shape, axis, which, first=0):
    p = lax.broadcasted_iota(jnp.int32, shape, axis) + first
    other = lax.broadcasted_iota(jnp.int32, shape, 1 - axis)
    return jnp.where(piece_places(p)[which] == other, 1.0, 0.0).astype(jnp.bfloat16)


def dot(a, b, dims=((1,), (0,))):
    return lax.dot_general(a, b, (dims, ((), ())), preferred_element_type=jnp.float32)


ROWS_BY_ROWS = ((1,), (1,))
COLS_BY_COLS = ((0,), (0,))


def lanes(index, size=QUAD):
    if isinstance(index, int):
        return pl.ds(index * size, size)
    return pl.ds(pl.multiple_of(index * size, size), size)


def kernel(
    x_hbm, do_hbm, gain_hbm, corner_hbm, wqkv_hbm, wout_hbm,
    mixed_o, scaled_o, inv_o,
    x_v, do_v, gain_v, corner_v, w_v, wo_v, pack_v, packt_v, west_v, east_v, spreadt_v,
    xn_v, xh_v, q_v, da_v, kvx_v, kt_v, mask_v, dk_v, dv_v,
    attf_v, gqf_v, att_v, g_v, gh1_v, gh2_v,
    score_v, prob_v, weight_v, dscore_v,
    edge1_v, rim1_r, edge1_r, send2a_v, recv2a_r, send2b_v, recv2b_r,
    in_sem, w_sem, send1_sem, recv1_sem, send2_sem, recv2_sem,
):
    f32, bf16 = jnp.float32, jnp.bfloat16
    lon, lev = lax.axis_index("lon"), lax.axis_index("lev")
    lons, levs = lax.axis_size("lon"), lax.axis_size("lev")
    target = [
        {"lon": lax.rem(lon + dx + lons, lons), "lev": lax.rem(lev + dy + levs, levs)}
        for dy, dx in AROUND
    ]
    barrier = pltpu.get_barrier_semaphore()
    for device in target:
        pl.semaphore_signal(
            barrier, inc=1, device_id=device, device_id_type=pl.DeviceIdType.MESH
        )

    small = [
        pltpu.make_async_copy(src, dst, in_sem.at[i])
        for i, (src, dst) in enumerate(
            [
                (x_hbm, x_v), (corner_hbm, corner_v), (gain_hbm, gain_v), (do_hbm, do_v),
            ]
        )
    ]
    for copy in small[:3]:
        copy.start()
    pack_v[...] = selection((PACK, CELLS), 0, 0)

    def weight(c):
        return pltpu.make_async_copy(wqkv_hbm.at[:, lanes(c)], w_v.at[:, lanes(c)], w_sem.at[c])

    out_weight = pltpu.make_async_copy(wout_hbm, wo_v, w_sem.at[3 * QUADS])

    def remote(src, dst, d, slot, send_sem, recv_sem):
        return pltpu.make_async_remote_copy(
            src_ref=src,
            dst_ref=dst,
            send_sem=send_sem.at[slot],
            recv_sem=recv_sem.at[slot],
            device_id=target[d],
            device_id_type=pl.DeviceIdType.MESH,
        )

    def rims(src, dst, slot, send_sem, recv_sem):
        return [
            remote(src[0], dst[1], 0, slot, send_sem, recv_sem),
            remote(src[1], dst[0], 1, slot + 1, send_sem, recv_sem),
        ]

    def pieces(src, dst, base, indices, slot, send_sem, recv_sem):
        copies = []
        for n, i in enumerate(indices):
            at, size = PIECES[i][1:]
            other = PIECES[OPPOSITE[2 + i] - 2][1]
            copies.append(
                remote(
                    src.at[pl.ds(base + at, size)], dst.at[pl.ds(base + other, size)], 2 + i,
                    slot + n, send_sem, recv_sem,
                )
            )
        return copies

    def halves(ref, half):
        columns = pl.ds(half * HALF, HALF)
        return [ref.at[pl.ds(0, RADIUS), columns], ref.at[pl.ds(ROWS - RADIUS, RADIUS), columns]]

    def arrivals(half):
        columns = pl.ds(half * HALF, HALF)
        return [rim1_r.at[pl.ds(0, RADIUS), columns], rim1_r.at[pl.ds(RADIUS, RADIUS), columns]]

    first = [
        rims(halves(x_hbm, p), arrivals(p), 5 * p, send1_sem, recv1_sem)
        + pieces(
            edge1_v, edge1_r, 0, (3, 4, 5) if p == 0 else (0, 1, 2), 5 * p + 2, send1_sem,
            recv1_sem,
        )
        for p in range(2)
    ]
    pl.semaphore_wait(barrier, len(target))
    for copy in first[0][:2]:
        copy.start()
    small[0].wait()
    x_own = x_v[...].reshape(CELLS, WIDTH)
    edge1_v[...] = dot(pack_v[...], x_own).astype(bf16)
    for copy in first[0][2:]:
        copy.start()
    for c in range(3 * QUADS):
        weight(c).start()
    small[3].start()
    out_weight.start()
    packt_v[...] = selection((CELLS, PACK), 1, 0)
    west_v[...] = selection((EDGE, SIDE), 1, 1)
    east_v[...] = selection((EDGE, SIDE), 1, 1, SIDE)
    spreadt_v[...] = selection((PACK, EDGE), 0, 1)

    small[1].wait()
    codes = corner_v[...].astype(f32).astype(bf16)
    key_at = lax.broadcasted_iota(jnp.int32, (SPAN, 128), 0)
    query_at = lax.broadcasted_iota(jnp.int32, (SPAN, 128), 1)
    ext_row, position = key_at >> 4, key_at & 15
    query_row, query_col = (query_at >> 3) & 7, query_at & 7
    key_col = jnp.where(position >= 13, position - 16, position)
    near_row = ext_row - RADIUS - query_row
    near_col = key_col - query_col
    key_row = lev * ROWS + ext_row - RADIUS
    fine = (
        (jnp.abs(near_row) <= RADIUS)
        & (jnp.abs(near_col) <= RADIUS)
        & ((position < 11) | (position > 12))
        & (key_row >= 0)
        & (key_row < levs * ROWS)
    )
    leaves = jnp.where(
        (near_row == 0) | (near_col == 0),
        -1,
        1 + jnp.where(near_row > 0, 2, 0) + jnp.where(near_col > 0, 1, 0),
    ).astype(f32)
    leaves = jnp.where(fine, leaves, -2.0)
    pick_col = lax.broadcasted_iota(jnp.int32, (COLS, 128), 0)
    pick_lane = lax.broadcasted_iota(jnp.int32, (COLS, 128), 1)
    row_of = lax.broadcasted_iota(jnp.int32, (ROWS, 128), 0)
    lane_row = (lax.broadcasted_iota(jnp.int32, (ROWS, 128), 1) >> 3) & 7
    for t in range(TILES):
        pick = jnp.where(pick_col == t * TILE + (pick_lane & 7), 1.0, 0.0).astype(bf16)
        spread_codes = dot(codes, pick)
        code = jnp.sum(
            jnp.where(row_of == lane_row, spread_codes, 0.0), axis=0, keepdims=True
        )
        mask_v[t] = jnp.where((leaves == code) | (leaves < -1.5), NEG, 0.0)

    small[2].wait()
    gain = gain_v[...]

    def normed(x):
        inv = lax.rsqrt(jnp.mean(x * x, axis=-1, keepdims=True) + EPSILON)
        return inv, (x * inv * gain).astype(bf16)

    inv_own, own = normed(x_own.astype(f32))
    xn_v[...] = own
    inv_o[...] = jnp.broadcast_to(inv_own, (CELLS, 128))

    def by_tiles(y):
        y = y.reshape(ROWS, TILES, TILE, QUAD)
        return jnp.concatenate([y[:, t] for t in range(TILES)], axis=0).reshape(CELLS, QUAD)

    @pl.loop(0, QUADS, unroll=True)
    def _(c):
        weight(c).wait()
        y = dot(xn_v[...], w_v[:, lanes(c)]) * (HEAD_DIM**-0.5)
        q_v[:, lanes(c)] = by_tiles(y).astype(bf16)

    for copy in first[1]:
        copy.start()

    @pl.loop(0, 2 * QUADS, unroll=True)
    def _(c):
        weight(QUADS + c).wait()
        y = dot(xn_v[...], w_v[:, lanes(QUADS + c)])
        kvx_v[pl.ds(RADIUS, ROWS), pl.ds(0, COLS), lanes(c)] = y.reshape(ROWS, COLS, QUAD)

    small[3].wait()
    out_weight.wait()

    @pl.loop(0, QUADS, unroll=True)
    def _(c):
        y = dot(do_v[...], wo_v[lanes(c), :], ROWS_BY_ROWS)
        da_v[:, lanes(c)] = by_tiles(y).astype(bf16)

    low_side = lax.broadcasted_iota(jnp.int32, (EXT, TILE, QUAD), 1) < 4

    def received(p, tiles):
        for copy in first[p]:
            copy.wait_recv()
        rim = rim1_r[:, pl.ds(p * HALF, HALF)].reshape(2 * RIM, WIDTH)
        xh_v[pl.ds(0, 2 * RIM)] = normed(rim.astype(f32))[1]
        edge = dot((east_v if p else west_v)[...], edge1_r[pl.ds(p * SIDE, SIDE)])
        xh_v[pl.ds(2 * RIM, EDGE)] = normed(edge)[1]

        @pl.loop(0, 2 * QUADS, unroll=True)
        def _(c):
            y = dot(xh_v[...], w_v[:, lanes(QUADS + c)])
            rim = y[: 2 * RIM].reshape(2, RADIUS, HALF, QUAD)
            kvx_v[pl.ds(0, RADIUS), pl.ds(p * HALF, HALF), lanes(c)] = rim[0]
            kvx_v[pl.ds(RADIUS + ROWS, RADIUS), pl.ds(p * HALF, HALF), lanes(c)] = rim[1]
            kvx_v[:, pl.ds(COLS + p * TILE, TILE), lanes(c)] = y[2 * RIM :].reshape(
                EXT, TILE, QUAD
            )
            for t in tiles:
                main = kvx_v[:, pl.ds(t * TILE, TILE), lanes(c)]
                east = kvx_v[:, pl.ds((t + 1 if t < TILES - 1 else TILES + 1) * TILE, TILE), lanes(c)]
                west = kvx_v[:, pl.ds((t - 1 if t > 0 else TILES) * TILE, TILE), lanes(c)]
                side = jnp.where(low_side, east, west)
                kt_v[t, :, lanes(c)] = (
                    jnp.concatenate([main, side], axis=1).reshape(SPAN, QUAD).astype(bf16)
                )

    lane_head = lax.broadcasted_iota(jnp.int32, (TILE * ROWS, QUAD), 1) >> 6
    head_masks = [jnp.where(lane_head == h, 1.0, 0.0).astype(bf16) for h in range(4)]

    def stacked(y):
        return jnp.concatenate([y * mask for mask in head_masks], axis=0)

    def unstacked(y):
        n = TILE * ROWS
        out = y[:n]
        for h in range(1, 4):
            out = jnp.where(lane_head == h, y[h * n : (h + 1) * n], out)
        return out.reshape(ROWS, TILE, QUAD)

    chunks = [pl.ds(r, 32) for r in range(0, SPAN, 32)]

    def folded(y):
        return jnp.sum(y.reshape(4, 8, QUAD), axis=0)

    def score(slot, t, j):
        key, value = kt_v[t, :, lanes(j)], kt_v[t, :, lanes(QUADS + j)]
        cells = pl.ds(t * TILE * ROWS, TILE * ROWS)
        query, d_attn = stacked(q_v[cells, lanes(j)]), stacked(da_v[cells, lanes(j)])
        score_v[slot] = dot(key, query, ROWS_BY_ROWS)
        prob_v[slot] = dot(value, d_attn, ROWS_BY_ROWS)

    def weigh(slot, t):
        total = jnp.zeros((8, QUAD), f32)
        for rows in chunks:
            mask = mask_v[t, rows]
            terms = jnp.exp(score_v[slot, rows] + jnp.concatenate([mask, mask], axis=1))
            score_v[slot, rows] = terms
            total += folded(terms)
        scale = 1.0 / jnp.sum(total, axis=0, keepdims=True)
        total = jnp.zeros((8, QUAD), f32)
        for rows in chunks:
            weights = score_v[slot, rows] * scale
            weight_v[slot, rows] = weights.astype(bf16)
            total += folded(weights * prob_v[slot, rows])
        delta = jnp.sum(total, axis=0, keepdims=True)
        for rows in chunks:
            weights = score_v[slot, rows] * scale
            dscore_v[slot, rows] = (weights * (prob_v[slot, rows] - delta)).astype(bf16)

    def apply(slot, t, j):
        key, value = kt_v[t, :, lanes(j)], kt_v[t, :, lanes(QUADS + j)]
        cells, columns = pl.ds(t * TILE * ROWS, TILE * ROWS), pl.ds(t * TILE, TILE)
        query, d_attn = stacked(q_v[cells, lanes(j)]), stacked(da_v[cells, lanes(j)])
        weights_b, dscore = weight_v[slot], dscore_v[slot]
        attf_v[:, columns, lanes(j)] = unstacked(dot(weights_b, value, COLS_BY_COLS))
        gqf_v[:, columns, lanes(j)] = unstacked(dot(dscore, key, COLS_BY_COLS)) * (
            HEAD_DIM**-0.5
        )
        dk_v[t, :, :, lanes(j)] = dot(dscore, query).reshape(EXT, 2 * TILE, QUAD)
        dv_v[t, :, :, lanes(j)] = dot(weights_b, d_attn).reshape(EXT, 2 * TILE, QUAD)

    def attend(items, after=None):
        for i in range(len(items) + 2):
            if i < len(items):
                score(i % 2, *items[i])
            if 0 <= i - 2:
                apply(i % 2, *items[i - 2])
                if after:
                    after(*items[i - 2])
            if 0 <= i - 1 < len(items):
                weigh((i - 1) % 2, items[i - 1][0])

    def gathered(j, half, gh_ref):
        for d_ref, block in ((dk_v, j), (dv_v, QUADS + j)):
            groups = []
            for t in (2 * half, 2 * half + 1):
                low = d_ref[t - 1, :, pl.ds(TILE, TILE), lanes(j)] if t > 0 else 0.0
                high = d_ref[t + 1, :, pl.ds(TILE, TILE), lanes(j)] if t < TILES - 1 else 0.0
                main = d_ref[t, :, pl.ds(0, TILE), lanes(j)]
                groups.append(main + jnp.where(low_side, low, high))
            whole = jnp.concatenate(groups, axis=1).astype(bf16)
            g_v[:, pl.ds(half * HALF, HALF), lanes(QUADS + block)] = whole[
                RADIUS : RADIUS + ROWS
            ]
            gh_ref[pl.ds(0, RIM), lanes(block)] = whole[:RADIUS].reshape(RIM, QUAD)
            gh_ref[pl.ds(RIM, RIM), lanes(block)] = whole[RADIUS + ROWS :].reshape(RIM, QUAD)
            if half == 1:
                east = d_ref[TILES - 1, :, pl.ds(TILE, TILE), lanes(j)]
                west = d_ref[0, :, pl.ds(TILE, TILE), lanes(j)]
                edge = jnp.where(low_side, east, west).reshape(EDGE, QUAD).astype(bf16)
                gh_ref[pl.ds(2 * RIM, PACK), lanes(block)] = dot(spreadt_v[...], edge).astype(bf16)

    def projected(gh_ref, out_ref):
        @pl.loop(0, QUADS, unroll=True)
        def _(n):
            y = dot(gh_ref[...], w_v[lanes(n), pl.ds(WIDTH, 2 * WIDTH)], ROWS_BY_ROWS)
            out_ref[:, lanes(n)] = y.astype(bf16)

    received(0, (0,))

    attend([(0, j) for j in range(QUADS)])
    received(1, (1, 2, 3))

    attend(
        [(t, j) for j in range(QUADS) for t in (1, 2)],
        lambda t, j: gathered(j, 0, gh1_v) if t == 2 else None,
    )
    projected(gh1_v, send2a_v)
    n_s = [pl.ds(0, RIM), pl.ds(RIM, RIM)]
    second = rims(
        [send2a_v.at[d] for d in n_s], [recv2a_r.at[d] for d in n_s], 0, send2_sem, recv2_sem
    )
    for copy in second:
        copy.start()

    attend([(3, j) for j in range(QUADS)], lambda t, j: gathered(j, 1, gh2_v))
    projected(gh2_v, send2b_v)
    third = rims(
        [send2b_v.at[d] for d in n_s], [recv2b_r.at[d] for d in n_s], 2, send2_sem, recv2_sem
    ) + pieces(send2b_v, recv2b_r, 2 * RIM, range(6), 4, send2_sem, recv2_sem)
    for copy in third:
        copy.start()

    att_v[...] = attf_v[...].astype(bf16).reshape(CELLS, WIDTH)
    g_v[:, :, pl.ds(0, WIDTH)] = gqf_v[...].astype(bf16)

    @pl.loop(0, QUADS, unroll=True)
    def _(n):
        mixed_o[:, lanes(n)] = dot(att_v[...], wo_v[:, lanes(n)]).astype(bf16)

    @pl.loop(0, QUADS, unroll=True)
    def _(n):
        scaled_o[:, lanes(n)] = dot(
            g_v[...].reshape(CELLS, 3 * WIDTH), w_v[lanes(n), :], ROWS_BY_ROWS
        )

    for copy in second + third:
        copy.wait_recv()

    def both(rows):
        west, east = (r[rows].astype(f32).reshape(RADIUS, HALF, WIDTH) for r in (recv2a_r, recv2b_r))
        return jnp.concatenate([west, east], axis=1).reshape(2 * RIM, WIDTH)

    scaled_o[pl.ds(0, 2 * RIM)] += both(n_s[0])
    scaled_o[pl.ds(CELLS - 2 * RIM, 2 * RIM)] += both(n_s[1])
    edges = dot(packt_v[...], recv2b_r[pl.ds(2 * RIM, PACK)])
    scaled_o[...] = (scaled_o[...] + edges) * gain
    for copy in first[0] + first[1] + second + third:
        copy.wait_send()


def finish(x_ref, mixed_ref, scaled_ref, inv_ref, mixed_hbm, gin_hbm, gin_v, sem):
    mixed_copy = pltpu.make_async_copy(mixed_ref, mixed_hbm, sem.at[0])
    mixed_copy.start()
    blocks = 4
    size = CELLS // blocks
    copies = []
    for b in range(blocks):
        rows = pl.ds(b * size, size)
        x, scaled, inv = x_ref[rows].astype(jnp.float32), scaled_ref[rows], inv_ref[rows][:, :1]
        mean = jnp.mean(x * scaled, axis=-1, keepdims=True)
        gin_v[rows] = (inv * scaled - x * (inv * inv * inv * mean)).astype(gin_v.dtype)
        copies.append(pltpu.make_async_copy(gin_v.at[rows], gin_hbm.at[rows], sem.at[1 + b]))
        copies[-1].start()
    for copy in [mixed_copy] + copies:
        copy.wait()


def shards(inputs, norm_gain, w_qkv, w_out, d_out, corner):
    assert inputs.shape == (ROWS, COLS, WIDTH), inputs.shape
    f32, bf16 = jnp.float32, jnp.bfloat16
    vmem, dma = pltpu.VMEM, pltpu.SemaphoreType.DMA
    anywhere = pl.BlockSpec(memory_space=pl.ANY)
    inside = pl.BlockSpec(memory_space=pltpu.VMEM)
    mixed, scaled, inv = pl.pallas_call(
        kernel,
        out_shape=[
            vmem((CELLS, WIDTH), bf16),
            vmem((CELLS, WIDTH), f32),
            vmem((CELLS, 128), f32),
        ],
        in_specs=[anywhere] * 6,
        out_specs=[inside] * 3,
        scratch_shapes=[
            vmem((ROWS, COLS, WIDTH), bf16),
            vmem((CELLS, WIDTH), bf16),
            vmem((1, WIDTH), f32),
            vmem((ROWS, COLS), jnp.int32),
            vmem((WIDTH, 3 * WIDTH), bf16),
            vmem((WIDTH, WIDTH), bf16),
            vmem((PACK, CELLS), bf16),
            vmem((CELLS, PACK), bf16),
            vmem((EDGE, SIDE), bf16),
            vmem((EDGE, SIDE), bf16),
            vmem((PACK, EDGE), bf16),
            vmem((CELLS, WIDTH), bf16),
            vmem((PART, WIDTH), bf16),
            vmem((CELLS, WIDTH), bf16),
            vmem((CELLS, WIDTH), bf16),
            vmem((EXT, COLS + 2 * TILE, 2 * WIDTH), f32),
            vmem((TILES, SPAN, 2 * WIDTH), bf16),
            vmem((TILES, SPAN, 128), f32),
            vmem((TILES, EXT, 2 * TILE, WIDTH), f32),
            vmem((TILES, EXT, 2 * TILE, WIDTH), f32),
            vmem((ROWS, COLS, WIDTH), f32),
            vmem((ROWS, COLS, WIDTH), f32),
            vmem((CELLS, WIDTH), bf16),
            vmem((ROWS, COLS, 3 * WIDTH), bf16),
            vmem((2 * RIM, 2 * WIDTH), bf16),
            vmem((LATE, 2 * WIDTH), bf16),
            vmem((2, SPAN, QUAD), f32),
            vmem((2, SPAN, QUAD), f32),
            vmem((2, SPAN, QUAD), bf16),
            vmem((2, SPAN, QUAD), bf16),
            vmem((PACK, WIDTH), bf16),
            vmem((2 * RADIUS, COLS, WIDTH), bf16),
            vmem((PACK, WIDTH), bf16),
            vmem((2 * RIM, WIDTH), bf16),
            vmem((2 * RIM, WIDTH), bf16),
            vmem((LATE, WIDTH), bf16),
            vmem((LATE, WIDTH), bf16),
            dma((4,)),
            dma((3 * QUADS + 1,)),
            dma((10,)),
            dma((10,)),
            dma((10,)),
            dma((10,)),
        ],
        compiler_params=pltpu.CompilerParams(
            collective_id=0, has_side_effects=True, vmem_limit_bytes=61 * 1024 * 1024
        ),
    )(
        inputs,
        d_out.reshape(CELLS, WIDTH),
        norm_gain.reshape(1, WIDTH),
        corner,
        w_qkv,
        w_out,
    )
    mixed_out, grad_input = pl.pallas_call(
        finish,
        out_shape=[jax.ShapeDtypeStruct((CELLS, WIDTH), bf16)] * 2,
        in_specs=[inside] * 4,
        out_specs=[anywhere] * 2,
        scratch_shapes=[vmem((CELLS, WIDTH), bf16), dma((5,))],
        compiler_params=pltpu.CompilerParams(vmem_limit_bytes=16 * 1024 * 1024),
    )(inputs.reshape(CELLS, WIDTH), mixed, scaled, inv)
    return mixed_out.reshape(inputs.shape), grad_input.reshape(inputs.shape)


def solution(mesh):
    placed = (P("lev", "lon", None), P(), P(), P(), P("lev", "lon", None), P("lev", "lon"))
    return jax.shard_map(
        shards,
        mesh=mesh,
        in_specs=placed,
        out_specs=(P("lev", "lon", None), P("lev", "lon", None)),
        check_vma=False,
    )
```

```python
import jax
import jax.numpy as jnp
from jax import lax
from jax.experimental import pallas as pl
from jax.experimental.pallas import tpu as pltpu
from jax.sharding import PartitionSpec as P

HEADS = 16
RADIUS = 3
EPSILON = 1e-06

ROWS, COLS, WIDTH = 8, 32, 1024
CELLS = ROWS * COLS
HEAD_DIM = WIDTH // HEADS
QUAD = 4 * HEAD_DIM
QUADS = WIDTH // QUAD
TILE = 8
TILES = COLS // TILE
EXT = ROWS + 2 * RADIUS
SPAN = EXT * 2 * TILE
HALF = COLS // 2
RIM = RADIUS * HALF
SIDE = 64
EDGE = EXT * TILE
PACK = 128
PART = 2 * RIM + EDGE
LATE = 2 * RIM + PACK
NEG = -1e30

PIECES = (
    ((0, -1), 0, 32),
    ((-1, -1), 32, 16),
    ((1, -1), 48, 16),
    ((0, 1), 64, 32),
    ((-1, 1), 96, 16),
    ((1, 1), 112, 16),
)
AROUND = ((-1, 0), (1, 0)) + tuple(p[0] for p in PIECES)
OPPOSITE = tuple(AROUND.index((-d[0], -d[1])) for d in AROUND)


def piece_places(p):
    east, r = p >> 6, p & 63
    north, south = (r >= 32) & (r < 48), r >= 48
    i = jnp.where(south, r - 48, jnp.where(north, r - 32, r))
    row = (i * 43) >> 7
    c = i - 3 * row
    valid = row < jnp.where(north | south, RADIUS, ROWS)
    own_row = row + jnp.where(south, ROWS - RADIUS, 0)
    ext_row = row + jnp.where(south, RADIUS + ROWS, jnp.where(north, 0, RADIUS))
    cell = own_row * COLS + c + (COLS - RADIUS) * east
    edge = ext_row * TILE + c + (TILE - RADIUS) * (1 - east)
    return jnp.where(valid, cell, -1), jnp.where(valid, edge, -1)


def selection(shape, axis, which, first=0):
    p = lax.broadcasted_iota(jnp.int32, shape, axis) + first
    other = lax.broadcasted_iota(jnp.int32, shape, 1 - axis)
    return jnp.where(piece_places(p)[which] == other, 1.0, 0.0).astype(jnp.bfloat16)


def dot(a, b, dims=((1,), (0,))):
    return lax.dot_general(a, b, (dims, ((), ())), preferred_element_type=jnp.float32)


ROWS_BY_ROWS = ((1,), (1,))
COLS_BY_COLS = ((0,), (0,))


def lanes(index, size=QUAD):
    if isinstance(index, int):
        return pl.ds(index * size, size)
    return pl.ds(pl.multiple_of(index * size, size), size)


def kernel(
    x_hbm, do_hbm, gain_hbm, corner_hbm, wqkv_hbm, wout_hbm,
    mixed_o, scaled_o, inv_o,
    x_v, do_v, gain_v, corner_v, w_v, wo_v, pack_v, packt_v, west_v, east_v, spreadt_v,
    xn_v, xh_v, q_v, da_v, kvx_v, kt_v, mask_v, dk_v, dv_v,
    attf_v, gqf_v, att_v, g_v, gh1_v, gh2_v,
    score_v, prob_v, weight_v, dscore_v,
    edge1_v, rim1_r, edge1_r, send2a_v, recv2a_r, send2b_v, recv2b_r,
    in_sem, w_sem, send1_sem, recv1_sem, send2_sem, recv2_sem,
):
    f32, bf16 = jnp.float32, jnp.bfloat16
    lon, lev = lax.axis_index("lon"), lax.axis_index("lev")
    lons, levs = lax.axis_size("lon"), lax.axis_size("lev")
    target = [
        {"lon": lax.rem(lon + dx + lons, lons), "lev": lax.rem(lev + dy + levs, levs)}
        for dy, dx in AROUND
    ]
    barrier = pltpu.get_barrier_semaphore()
    for device in target:
        pl.semaphore_signal(
            barrier, inc=1, device_id=device, device_id_type=pl.DeviceIdType.MESH
        )

    small = [
        pltpu.make_async_copy(src, dst, in_sem.at[i])
        for i, (src, dst) in enumerate(
            [
                (x_hbm, x_v), (corner_hbm, corner_v), (gain_hbm, gain_v), (do_hbm, do_v),
            ]
        )
    ]
    for copy in small[:3]:
        copy.start()
    pack_v[...] = selection((PACK, CELLS), 0, 0)

    def weight(c):
        return pltpu.make_async_copy(wqkv_hbm.at[:, lanes(c)], w_v.at[:, lanes(c)], w_sem.at[c])

    out_weight = pltpu.make_async_copy(wout_hbm, wo_v, w_sem.at[3 * QUADS])

    def remote(src, dst, d, slot, send_sem, recv_sem):
        return pltpu.make_async_remote_copy(
            src_ref=src,
            dst_ref=dst,
            send_sem=send_sem.at[slot],
            recv_sem=recv_sem.at[slot],
            device_id=target[d],
            device_id_type=pl.DeviceIdType.MESH,
        )

    def rims(src, dst, slot, send_sem, recv_sem):
        return [
            remote(src[0], dst[1], 0, slot, send_sem, recv_sem),
            remote(src[1], dst[0], 1, slot + 1, send_sem, recv_sem),
        ]

    def pieces(src, dst, base, indices, slot, send_sem, recv_sem):
        copies = []
        for n, i in enumerate(indices):
            at, size = PIECES[i][1:]
            other = PIECES[OPPOSITE[2 + i] - 2][1]
            copies.append(
                remote(
                    src.at[pl.ds(base + at, size)], dst.at[pl.ds(base + other, size)], 2 + i,
                    slot + n, send_sem, recv_sem,
                )
            )
        return copies

    def halves(ref, half):
        columns = pl.ds(half * HALF, HALF)
        return [ref.at[pl.ds(0, RADIUS), columns], ref.at[pl.ds(ROWS - RADIUS, RADIUS), columns]]

    def arrivals(half):
        columns = pl.ds(half * HALF, HALF)
        return [rim1_r.at[pl.ds(0, RADIUS), columns], rim1_r.at[pl.ds(RADIUS, RADIUS), columns]]

    first = [
        rims(halves(x_hbm, p), arrivals(p), 5 * p, send1_sem, recv1_sem)
        + pieces(
            edge1_v, edge1_r, 0, (3, 4, 5) if p == 0 else (0, 1, 2), 5 * p + 2, send1_sem,
            recv1_sem,
        )
        for p in range(2)
    ]
    pl.semaphore_wait(barrier, len(target))
    for copy in first[0][:2]:
        copy.start()
    small[0].wait()
    x_own = x_v[...].reshape(CELLS, WIDTH)
    edge1_v[...] = dot(pack_v[...], x_own).astype(bf16)
    for copy in first[0][2:]:
        copy.start()
    for c in range(3 * QUADS):
        weight(c).start()
    small[3].start()
    out_weight.start()
    packt_v[...] = selection((CELLS, PACK), 1, 0)
    west_v[...] = selection((EDGE, SIDE), 1, 1)
    east_v[...] = selection((EDGE, SIDE), 1, 1, SIDE)
    spreadt_v[...] = selection((PACK, EDGE), 0, 1)

    small[1].wait()
    codes = corner_v[...].astype(f32).astype(bf16)
    key_at = lax.broadcasted_iota(jnp.int32, (SPAN, 128), 0)
    query_at = lax.broadcasted_iota(jnp.int32, (SPAN, 128), 1)
    ext_row, position = key_at >> 4, key_at & 15
    query_row, query_col = (query_at >> 3) & 7, query_at & 7
    key_col = jnp.where(position >= 13, position - 16, position)
    near_row = ext_row - RADIUS - query_row
    near_col = key_col - query_col
    key_row = lev * ROWS + ext_row - RADIUS
    fine = (
        (jnp.abs(near_row) <= RADIUS)
        & (jnp.abs(near_col) <= RADIUS)
        & ((position < 11) | (position > 12))
        & (key_row >= 0)
        & (key_row < levs * ROWS)
    )
    leaves = jnp.where(
        (near_row == 0) | (near_col == 0),
        -1,
        1 + jnp.where(near_row > 0, 2, 0) + jnp.where(near_col > 0, 1, 0),
    ).astype(f32)
    leaves = jnp.where(fine, leaves, -2.0)
    pick_col = lax.broadcasted_iota(jnp.int32, (COLS, 128), 0)
    pick_lane = lax.broadcasted_iota(jnp.int32, (COLS, 128), 1)
    row_of = lax.broadcasted_iota(jnp.int32, (ROWS, 128), 0)
    lane_row = (lax.broadcasted_iota(jnp.int32, (ROWS, 128), 1) >> 3) & 7
    for t in range(TILES):
        pick = jnp.where(pick_col == t * TILE + (pick_lane & 7), 1.0, 0.0).astype(bf16)
        spread_codes = dot(codes, pick)
        code = jnp.sum(
            jnp.where(row_of == lane_row, spread_codes, 0.0), axis=0, keepdims=True
        )
        mask_v[t] = jnp.where((leaves == code) | (leaves < -1.5), NEG, 0.0)

    small[2].wait()
    gain = gain_v[...]

    def normed(x):
        inv = lax.rsqrt(jnp.mean(x * x, axis=-1, keepdims=True) + EPSILON)
        return inv, (x * inv * gain).astype(bf16)

    inv_own, own = normed(x_own.astype(f32))
    xn_v[...] = own
    inv_o[...] = jnp.broadcast_to(inv_own, (CELLS, 128))

    def by_tiles(y):
        y = y.reshape(ROWS, TILES, TILE, QUAD)
        return jnp.concatenate([y[:, t] for t in range(TILES)], axis=0).reshape(CELLS, QUAD)

    for c in range(QUADS):
        weight(c).wait()
    for c in range(QUADS):
        y = dot(xn_v[...], w_v[:, lanes(c)]) * (HEAD_DIM**-0.5)
        q_v[:, lanes(c)] = by_tiles(y).astype(bf16)

    for copy in first[1]:
        copy.start()

    for c in range(QUADS, 3 * QUADS):
        weight(c).wait()
    for c in range(2 * QUADS):
        y = dot(xn_v[...], w_v[:, lanes(QUADS + c)])
        kvx_v[pl.ds(RADIUS, ROWS), pl.ds(0, COLS), lanes(c)] = y.reshape(ROWS, COLS, QUAD)

    small[3].wait()
    out_weight.wait()

    @pl.loop(0, QUADS, unroll=True)
    def _(c):
        y = dot(do_v[...], wo_v[lanes(c), :], ROWS_BY_ROWS)
        da_v[:, lanes(c)] = by_tiles(y).astype(bf16)

    low_side = lax.broadcasted_iota(jnp.int32, (EXT, TILE, QUAD), 1) < 4

    def received(p, tiles):
        for copy in first[p]:
            copy.wait_recv()
        rim = rim1_r[:, pl.ds(p * HALF, HALF)].reshape(2 * RIM, WIDTH)
        xh_v[pl.ds(0, 2 * RIM)] = normed(rim.astype(f32))[1]
        edge = dot((east_v if p else west_v)[...], edge1_r[pl.ds(p * SIDE, SIDE)])
        xh_v[pl.ds(2 * RIM, EDGE)] = normed(edge)[1]

        @pl.loop(0, 2 * QUADS, unroll=True)
        def _(c):
            y = dot(xh_v[...], w_v[:, lanes(QUADS + c)])
            rim = y[: 2 * RIM].reshape(2, RADIUS, HALF, QUAD)
            kvx_v[pl.ds(0, RADIUS), pl.ds(p * HALF, HALF), lanes(c)] = rim[0]
            kvx_v[pl.ds(RADIUS + ROWS, RADIUS), pl.ds(p * HALF, HALF), lanes(c)] = rim[1]
            kvx_v[:, pl.ds(COLS + p * TILE, TILE), lanes(c)] = y[2 * RIM :].reshape(
                EXT, TILE, QUAD
            )
            for t in tiles:
                main = kvx_v[:, pl.ds(t * TILE, TILE), lanes(c)]
                east = kvx_v[:, pl.ds((t + 1 if t < TILES - 1 else TILES + 1) * TILE, TILE), lanes(c)]
                west = kvx_v[:, pl.ds((t - 1 if t > 0 else TILES) * TILE, TILE), lanes(c)]
                side = jnp.where(low_side, east, west)
                kt_v[t, :, lanes(c)] = (
                    jnp.concatenate([main, side], axis=1).reshape(SPAN, QUAD).astype(bf16)
                )

    lane_head = lax.broadcasted_iota(jnp.int32, (TILE * ROWS, QUAD), 1) >> 6
    head_masks = [jnp.where(lane_head == h, 1.0, 0.0).astype(bf16) for h in range(4)]

    def stacked(y):
        return jnp.concatenate([y * mask for mask in head_masks], axis=0)

    def unstacked(y):
        n = TILE * ROWS
        out = y[:n]
        for h in range(1, 4):
            out = jnp.where(lane_head == h, y[h * n : (h + 1) * n], out)
        return out.reshape(ROWS, TILE, QUAD)

    chunks = [pl.ds(r, 32) for r in range(0, SPAN, 32)]

    def folded(y):
        return jnp.sum(y.reshape(4, 8, QUAD), axis=0)

    def score(slot, t, j):
        key, value = kt_v[t, :, lanes(j)], kt_v[t, :, lanes(QUADS + j)]
        cells = pl.ds(t * TILE * ROWS, TILE * ROWS)
        query, d_attn = stacked(q_v[cells, lanes(j)]), stacked(da_v[cells, lanes(j)])
        score_v[slot] = dot(key, query, ROWS_BY_ROWS)
        prob_v[slot] = dot(value, d_attn, ROWS_BY_ROWS)

    def weigh(slot, i, t):
        total = jnp.zeros((8, QUAD), f32)
        for rows in chunks:
            mask = mask_v[t, rows]
            terms = jnp.exp(score_v[slot, rows] + jnp.concatenate([mask, mask], axis=1))
            score_v[slot, rows] = terms
            total += folded(terms)
        scale = 1.0 / jnp.sum(total, axis=0, keepdims=True)
        total = jnp.zeros((8, QUAD), f32)
        for rows in chunks:
            weights = score_v[slot, rows] * scale
            weight_v[i, rows] = weights.astype(bf16)
            total += folded(weights * prob_v[slot, rows])
        delta = jnp.sum(total, axis=0, keepdims=True)
        for rows in chunks:
            weights = score_v[slot, rows] * scale
            dscore_v[i, rows] = (weights * (prob_v[slot, rows] - delta)).astype(bf16)

    def to_keys(i, t, j):
        cells = pl.ds(t * TILE * ROWS, TILE * ROWS)
        query, d_attn = stacked(q_v[cells, lanes(j)]), stacked(da_v[cells, lanes(j)])
        dk_v[t, :, :, lanes(j)] = dot(dscore_v[i], query).reshape(EXT, 2 * TILE, QUAD)
        dv_v[t, :, :, lanes(j)] = dot(weight_v[i], d_attn).reshape(EXT, 2 * TILE, QUAD)

    def to_queries(i, t, j):
        key, value = kt_v[t, :, lanes(j)], kt_v[t, :, lanes(QUADS + j)]
        columns = pl.ds(t * TILE, TILE)
        attf_v[:, columns, lanes(j)] = unstacked(dot(weight_v[i].T, value))
        gqf_v[:, columns, lanes(j)] = unstacked(dot(dscore_v[i].T, key)) * (
            HEAD_DIM**-0.5
        )

    def attend(items, before, after):
        for i in range(len(items) + 2):
            if i < len(items):
                before(*items[i])
                score(i % 2, *items[i])
            if 0 <= i - 2:
                to_keys(i - 2, *items[i - 2])
                after(*items[i - 2])
            if 0 <= i - 1 < len(items):
                weigh((i - 1) % 2, i - 1, items[i - 1][0])

    def gathered(j, half, gh_ref):
        for d_ref, block in ((dk_v, j), (dv_v, QUADS + j)):
            groups = []
            for t in (2 * half, 2 * half + 1):
                low = d_ref[t - 1, :, pl.ds(TILE, TILE), lanes(j)] if t > 0 else 0.0
                high = d_ref[t + 1, :, pl.ds(TILE, TILE), lanes(j)] if t < TILES - 1 else 0.0
                main = d_ref[t, :, pl.ds(0, TILE), lanes(j)]
                groups.append(main + jnp.where(low_side, low, high))
            whole = jnp.concatenate(groups, axis=1).astype(bf16)
            g_v[:, pl.ds(half * HALF, HALF), lanes(QUADS + block)] = whole[
                RADIUS : RADIUS + ROWS
            ]
            gh_ref[pl.ds(0, RIM), lanes(block)] = whole[:RADIUS].reshape(RIM, QUAD)
            gh_ref[pl.ds(RIM, RIM), lanes(block)] = whole[RADIUS + ROWS :].reshape(RIM, QUAD)
            if half == 1:
                east = d_ref[TILES - 1, :, pl.ds(TILE, TILE), lanes(j)]
                west = d_ref[0, :, pl.ds(TILE, TILE), lanes(j)]
                edge = jnp.where(low_side, east, west).reshape(EDGE, QUAD).astype(bf16)
                gh_ref[pl.ds(2 * RIM, PACK), lanes(block)] = dot(spreadt_v[...], edge).astype(bf16)

    def projected(gh_ref, out_ref):
        @pl.loop(0, QUADS, unroll=True)
        def _(n):
            y = dot(gh_ref[...], w_v[lanes(n), pl.ds(WIDTH, 2 * WIDTH)], ROWS_BY_ROWS)
            out_ref[:, lanes(n)] = y.astype(bf16)

    n_s = [pl.ds(0, RIM), pl.ds(RIM, RIM)]
    second = rims(
        [send2a_v.at[d] for d in n_s], [recv2a_r.at[d] for d in n_s], 0, send2_sem, recv2_sem
    )
    third = rims(
        [send2b_v.at[d] for d in n_s], [recv2b_r.at[d] for d in n_s], 2, send2_sem, recv2_sem
    ) + pieces(send2b_v, recv2b_r, 2 * RIM, range(6), 4, send2_sem, recv2_sem)

    def before(t, j):
        if (t, j) == (0, 0):
            received(0, (0,))
        if (t, j) == (1, 0):
            received(1, (1, 2, 3))

    def after(t, j):
        if t == 2:
            gathered(j, 0, gh1_v)
        if t == 3:
            gathered(j, 1, gh2_v)
        if (t, j) == (2, QUADS - 1):
            projected(gh1_v, send2a_v)
            for copy in second:
                copy.start()

    items = (
        [(0, j) for j in range(QUADS)]
        + [(t, j) for j in range(QUADS) for t in (1, 2)]
        + [(3, j) for j in range(QUADS)]
    )
    attend(items, before, after)
    projected(gh2_v, send2b_v)
    for copy in third:
        copy.start()

    for n in range(QUADS):
        for i in range(n * len(items) // QUADS, (n + 1) * len(items) // QUADS):
            to_queries(i, *items[i])
        scaled_o[:, lanes(n)] = dot(
            g_v[:, :, pl.ds(WIDTH, 2 * WIDTH)].reshape(CELLS, 2 * WIDTH),
            w_v[lanes(n), pl.ds(WIDTH, 2 * WIDTH)],
            ROWS_BY_ROWS,
        )
    att_v[...] = attf_v[...].astype(bf16).reshape(CELLS, WIDTH)
    g_v[:, :, pl.ds(0, WIDTH)] = gqf_v[...].astype(bf16)
    for n in range(QUADS):
        mixed_o[:, lanes(n)] = dot(att_v[...], wo_v[:, lanes(n)]).astype(bf16)
        scaled_o[:, lanes(n)] += dot(
            g_v[:, :, pl.ds(0, WIDTH)].reshape(CELLS, WIDTH),
            w_v[lanes(n), pl.ds(0, WIDTH)],
            ROWS_BY_ROWS,
        )

    for copy in second + third:
        copy.wait_recv()

    def both(rows):
        west, east = (r[rows].astype(f32).reshape(RADIUS, HALF, WIDTH) for r in (recv2a_r, recv2b_r))
        return jnp.concatenate([west, east], axis=1).reshape(2 * RIM, WIDTH)

    scaled_o[pl.ds(0, 2 * RIM)] += both(n_s[0])
    scaled_o[pl.ds(CELLS - 2 * RIM, 2 * RIM)] += both(n_s[1])
    edges = dot(packt_v[...], recv2b_r[pl.ds(2 * RIM, PACK)])
    scaled_o[...] = (scaled_o[...] + edges) * gain
    for copy in first[0] + first[1] + second + third:
        copy.wait_send()


def finish(x_ref, mixed_ref, scaled_ref, inv_ref, mixed_hbm, gin_hbm, gin_v, sem):
    mixed_copy = pltpu.make_async_copy(mixed_ref, mixed_hbm, sem.at[0])
    mixed_copy.start()
    blocks = 4
    size = CELLS // blocks
    copies = []
    for b in range(blocks):
        rows = pl.ds(b * size, size)
        x, scaled, inv = x_ref[rows].astype(jnp.float32), scaled_ref[rows], inv_ref[rows][:, :1]
        mean = jnp.mean(x * scaled, axis=-1, keepdims=True)
        gin_v[rows] = (inv * scaled - x * (inv * inv * inv * mean)).astype(gin_v.dtype)
        copies.append(pltpu.make_async_copy(gin_v.at[rows], gin_hbm.at[rows], sem.at[1 + b]))
        copies[-1].start()
    for copy in [mixed_copy] + copies:
        copy.wait()


def shards(inputs, norm_gain, w_qkv, w_out, d_out, corner):
    assert inputs.shape == (ROWS, COLS, WIDTH), inputs.shape
    f32, bf16 = jnp.float32, jnp.bfloat16
    vmem, dma = pltpu.VMEM, pltpu.SemaphoreType.DMA
    anywhere = pl.BlockSpec(memory_space=pl.ANY)
    inside = pl.BlockSpec(memory_space=pltpu.VMEM)
    mixed, scaled, inv = pl.pallas_call(
        kernel,
        out_shape=[
            vmem((CELLS, WIDTH), bf16),
            vmem((CELLS, WIDTH), f32),
            vmem((CELLS, 128), f32),
        ],
        in_specs=[anywhere] * 6,
        out_specs=[inside] * 3,
        scratch_shapes=[
            vmem((ROWS, COLS, WIDTH), bf16),
            vmem((CELLS, WIDTH), bf16),
            vmem((1, WIDTH), f32),
            vmem((ROWS, COLS), jnp.int32),
            vmem((WIDTH, 3 * WIDTH), bf16),
            vmem((WIDTH, WIDTH), bf16),
            vmem((PACK, CELLS), bf16),
            vmem((CELLS, PACK), bf16),
            vmem((EDGE, SIDE), bf16),
            vmem((EDGE, SIDE), bf16),
            vmem((PACK, EDGE), bf16),
            vmem((CELLS, WIDTH), bf16),
            vmem((PART, WIDTH), bf16),
            vmem((CELLS, WIDTH), bf16),
            vmem((CELLS, WIDTH), bf16),
            vmem((EXT, COLS + 2 * TILE, 2 * WIDTH), f32),
            vmem((TILES, SPAN, 2 * WIDTH), bf16),
            vmem((TILES, SPAN, 128), f32),
            vmem((TILES, EXT, 2 * TILE, WIDTH), f32),
            vmem((TILES, EXT, 2 * TILE, WIDTH), f32),
            vmem((ROWS, COLS, WIDTH), f32),
            vmem((ROWS, COLS, WIDTH), f32),
            vmem((CELLS, WIDTH), bf16),
            vmem((ROWS, COLS, 3 * WIDTH), bf16),
            vmem((2 * RIM, 2 * WIDTH), bf16),
            vmem((LATE, 2 * WIDTH), bf16),
            vmem((2, SPAN, QUAD), f32),
            vmem((2, SPAN, QUAD), f32),
            vmem((TILES * QUADS, SPAN, QUAD), bf16),
            vmem((TILES * QUADS, SPAN, QUAD), bf16),
            vmem((PACK, WIDTH), bf16),
            vmem((2 * RADIUS, COLS, WIDTH), bf16),
            vmem((PACK, WIDTH), bf16),
            vmem((2 * RIM, WIDTH), bf16),
            vmem((2 * RIM, WIDTH), bf16),
            vmem((LATE, WIDTH), bf16),
            vmem((LATE, WIDTH), bf16),
            dma((4,)),
            dma((3 * QUADS + 1,)),
            dma((10,)),
            dma((10,)),
            dma((10,)),
            dma((10,)),
        ],
        compiler_params=pltpu.CompilerParams(
            collective_id=0, has_side_effects=True, vmem_limit_bytes=61 * 1024 * 1024
        ),
    )(
        inputs,
        d_out.reshape(CELLS, WIDTH),
        norm_gain.reshape(1, WIDTH),
        corner,
        w_qkv,
        w_out,
    )
    mixed_out, grad_input = pl.pallas_call(
        finish,
        out_shape=[jax.ShapeDtypeStruct((CELLS, WIDTH), bf16)] * 2,
        in_specs=[inside] * 4,
        out_specs=[anywhere] * 2,
        scratch_shapes=[vmem((CELLS, WIDTH), bf16), dma((5,))],
        compiler_params=pltpu.CompilerParams(vmem_limit_bytes=16 * 1024 * 1024),
    )(inputs.reshape(CELLS, WIDTH), mixed, scaled, inv)
    return mixed_out.reshape(inputs.shape), grad_input.reshape(inputs.shape)


def solution(mesh):
    placed = (P("lev", "lon", None), P(), P(), P(), P("lev", "lon", None), P("lev", "lon"))
    return jax.shard_map(
        shards,
        mesh=mesh,
        in_specs=placed,
        out_specs=(P("lev", "lon", None), P("lev", "lon", None)),
        check_vma=False,
    )
```

```python
import jax
import jax.numpy as jnp
from jax import lax
from jax.experimental import pallas as pl
from jax.experimental.pallas import tpu as pltpu
from jax.sharding import PartitionSpec as P

HEADS = 16
RADIUS = 3
EPSILON = 1e-06

ROWS, COLS, WIDTH = 8, 32, 1024
CELLS = ROWS * COLS
HEAD_DIM = WIDTH // HEADS
QUAD = 4 * HEAD_DIM
QUADS = WIDTH // QUAD
TILE = 8
TILES = COLS // TILE
EXT = ROWS + 2 * RADIUS
SPAN = EXT * 2 * TILE
HALF = COLS // 2
RIM = RADIUS * HALF
SIDE = 64
EDGE = EXT * TILE
PACK = 128
PART = 2 * RIM + EDGE
LATE = 2 * RIM + PACK
NEG = -1e30

PIECES = (
    ((0, -1), 0, 32),
    ((-1, -1), 32, 16),
    ((1, -1), 48, 16),
    ((0, 1), 64, 32),
    ((-1, 1), 96, 16),
    ((1, 1), 112, 16),
)
AROUND = ((-1, 0), (1, 0)) + tuple(p[0] for p in PIECES)
OPPOSITE = tuple(AROUND.index((-d[0], -d[1])) for d in AROUND)


def piece_places(p):
    east, r = p >> 6, p & 63
    north, south = (r >= 32) & (r < 48), r >= 48
    i = jnp.where(south, r - 48, jnp.where(north, r - 32, r))
    row = (i * 43) >> 7
    c = i - 3 * row
    valid = row < jnp.where(north | south, RADIUS, ROWS)
    own_row = row + jnp.where(south, ROWS - RADIUS, 0)
    ext_row = row + jnp.where(south, RADIUS + ROWS, jnp.where(north, 0, RADIUS))
    cell = own_row * COLS + c + (COLS - RADIUS) * east
    edge = ext_row * TILE + c + (TILE - RADIUS) * (1 - east)
    return jnp.where(valid, cell, -1), jnp.where(valid, edge, -1)


def selection(shape, axis, which, first=0):
    p = lax.broadcasted_iota(jnp.int32, shape, axis) + first
    other = lax.broadcasted_iota(jnp.int32, shape, 1 - axis)
    return jnp.where(piece_places(p)[which] == other, 1.0, 0.0).astype(jnp.bfloat16)


def dot(a, b, dims=((1,), (0,))):
    return lax.dot_general(a, b, (dims, ((), ())), preferred_element_type=jnp.float32)


ROWS_BY_ROWS = ((1,), (1,))
COLS_BY_COLS = ((0,), (0,))


def lanes(index, size=QUAD):
    if isinstance(index, int):
        return pl.ds(index * size, size)
    return pl.ds(pl.multiple_of(index * size, size), size)


def kernel(
    x_hbm, do_hbm, gain_hbm, corner_hbm, wqkv_hbm, wout_hbm,
    mixed_o, scaled_o, inv_o,
    x_v, do_v, gain_v, corner_v, w_v, wo_v, pack_v, packt_v, west_v, east_v, spreadt_v,
    xn_v, xh_v, q_v, da_v, kvx_v, kt_v, mask_v, dk_v, dv_v,
    attf_v, gqf_v, att_v, g_v, gh1_v, gh2_v,
    score_v, prob_v, weight_v, dscore_v,
    edge1_v, rim1_r, edge1_r, send2a_v, recv2a_r, send2b_v, recv2b_r,
    in_sem, w_sem, send1_sem, recv1_sem, send2_sem, recv2_sem,
):
    f32, bf16 = jnp.float32, jnp.bfloat16
    lon, lev = lax.axis_index("lon"), lax.axis_index("lev")
    lons, levs = lax.axis_size("lon"), lax.axis_size("lev")
    target = [
        {"lon": lax.rem(lon + dx + lons, lons), "lev": lax.rem(lev + dy + levs, levs)}
        for dy, dx in AROUND
    ]
    barrier = pltpu.get_barrier_semaphore()
    for device in target:
        pl.semaphore_signal(
            barrier, inc=1, device_id=device, device_id_type=pl.DeviceIdType.MESH
        )

    small = [
        pltpu.make_async_copy(src, dst, in_sem.at[i])
        for i, (src, dst) in enumerate(
            [
                (x_hbm, x_v), (corner_hbm, corner_v), (gain_hbm, gain_v), (do_hbm, do_v),
            ]
        )
    ]
    for copy in small[:3]:
        copy.start()
    pack_v[...] = selection((PACK, CELLS), 0, 0)

    def weight(c):
        return pltpu.make_async_copy(wqkv_hbm.at[:, lanes(c)], w_v.at[:, lanes(c)], w_sem.at[c])

    out_weight = pltpu.make_async_copy(wout_hbm, wo_v, w_sem.at[3 * QUADS])

    def remote(src, dst, d, slot, send_sem, recv_sem):
        return pltpu.make_async_remote_copy(
            src_ref=src,
            dst_ref=dst,
            send_sem=send_sem.at[slot],
            recv_sem=recv_sem.at[slot],
            device_id=target[d],
            device_id_type=pl.DeviceIdType.MESH,
        )

    def rims(src, dst, slot, send_sem, recv_sem):
        return [
            remote(src[0], dst[1], 0, slot, send_sem, recv_sem),
            remote(src[1], dst[0], 1, slot + 1, send_sem, recv_sem),
        ]

    def pieces(src, dst, base, indices, slot, send_sem, recv_sem):
        copies = []
        for n, i in enumerate(indices):
            at, size = PIECES[i][1:]
            other = PIECES[OPPOSITE[2 + i] - 2][1]
            copies.append(
                remote(
                    src.at[pl.ds(base + at, size)], dst.at[pl.ds(base + other, size)], 2 + i,
                    slot + n, send_sem, recv_sem,
                )
            )
        return copies

    def halves(ref, half):
        columns = pl.ds(half * HALF, HALF)
        return [ref.at[pl.ds(0, RADIUS), columns], ref.at[pl.ds(ROWS - RADIUS, RADIUS), columns]]

    def arrivals(half):
        columns = pl.ds(half * HALF, HALF)
        return [rim1_r.at[pl.ds(0, RADIUS), columns], rim1_r.at[pl.ds(RADIUS, RADIUS), columns]]

    first = [
        rims(halves(x_hbm, p), arrivals(p), 5 * p, send1_sem, recv1_sem)
        + pieces(
            edge1_v, edge1_r, 0, (3, 4, 5) if p == 0 else (0, 1, 2), 5 * p + 2, send1_sem,
            recv1_sem,
        )
        for p in range(2)
    ]
    for c in range(2 * QUADS):
        weight(c).start()
    small[0].wait()
    x_own = x_v[...].reshape(CELLS, WIDTH)
    edge1_v[...] = dot(pack_v[...], x_own).astype(bf16)
    pl.semaphore_wait(barrier, len(target))
    for copy in first[0] + first[1]:
        copy.start()
    for c in range(2 * QUADS, 3 * QUADS):
        weight(c).start()
    small[3].start()
    out_weight.start()
    packt_v[...] = selection((CELLS, PACK), 1, 0)
    west_v[...] = selection((EDGE, SIDE), 1, 1)
    east_v[...] = selection((EDGE, SIDE), 1, 1, SIDE)
    spreadt_v[...] = selection((PACK, EDGE), 0, 1)

    small[1].wait()
    codes = corner_v[...].astype(f32).astype(bf16)
    key_at = lax.broadcasted_iota(jnp.int32, (SPAN, 128), 0)
    query_at = lax.broadcasted_iota(jnp.int32, (SPAN, 128), 1)
    ext_row, position = key_at >> 4, key_at & 15
    query_row, query_col = (query_at >> 3) & 7, query_at & 7
    key_col = jnp.where(position >= 13, position - 16, position)
    near_row = ext_row - RADIUS - query_row
    near_col = key_col - query_col
    key_row = lev * ROWS + ext_row - RADIUS
    fine = (
        (jnp.abs(near_row) <= RADIUS)
        & (jnp.abs(near_col) <= RADIUS)
        & ((position < 11) | (position > 12))
        & (key_row >= 0)
        & (key_row < levs * ROWS)
    )
    leaves = jnp.where(
        (near_row == 0) | (near_col == 0),
        -1,
        1 + jnp.where(near_row > 0, 2, 0) + jnp.where(near_col > 0, 1, 0),
    ).astype(f32)
    leaves = jnp.where(fine, leaves, -2.0)
    pick_col = lax.broadcasted_iota(jnp.int32, (COLS, 128), 0)
    pick_lane = lax.broadcasted_iota(jnp.int32, (COLS, 128), 1)
    row_of = lax.broadcasted_iota(jnp.int32, (ROWS, 128), 0)
    lane_row = (lax.broadcasted_iota(jnp.int32, (ROWS, 128), 1) >> 3) & 7
    for t in range(TILES):
        pick = jnp.where(pick_col == t * TILE + (pick_lane & 7), 1.0, 0.0).astype(bf16)
        spread_codes = dot(codes, pick)
        code = jnp.sum(
            jnp.where(row_of == lane_row, spread_codes, 0.0), axis=0, keepdims=True
        )
        mask_v[t] = jnp.where((leaves == code) | (leaves < -1.5), NEG, 0.0)

    small[2].wait()
    gain = gain_v[...]

    def normed(x):
        inv = lax.rsqrt(jnp.mean(x * x, axis=-1, keepdims=True) + EPSILON)
        return inv, (x * inv * gain).astype(bf16)

    inv_own, own = normed(x_own.astype(f32))
    xn_v[...] = own
    inv_o[...] = jnp.broadcast_to(inv_own, (CELLS, 128))

    def by_tiles(y):
        y = y.reshape(ROWS, TILES, TILE, QUAD)
        return jnp.concatenate([y[:, t] for t in range(TILES)], axis=0).reshape(CELLS, QUAD)

    for c in range(QUADS):
        weight(c).wait()
    for c in range(QUADS):
        y = dot(xn_v[...], w_v[:, lanes(c)]) * (HEAD_DIM**-0.5)
        q_v[:, lanes(c)] = by_tiles(y).astype(bf16)

    for c in range(QUADS, 3 * QUADS):
        weight(c).wait()
    for c in range(2 * QUADS):
        y = dot(xn_v[...], w_v[:, lanes(QUADS + c)])
        kvx_v[pl.ds(RADIUS, ROWS), pl.ds(0, COLS), lanes(c)] = y.reshape(ROWS, COLS, QUAD)

    small[3].wait()
    out_weight.wait()

    @pl.loop(0, QUADS, unroll=True)
    def _(c):
        y = dot(do_v[...], wo_v[lanes(c), :], ROWS_BY_ROWS)
        da_v[:, lanes(c)] = by_tiles(y).astype(bf16)

    low_side = lax.broadcasted_iota(jnp.int32, (EXT, TILE, QUAD), 1) < 4

    def received(p, tiles):
        for copy in first[p]:
            copy.wait_recv()
        rim = rim1_r[:, pl.ds(p * HALF, HALF)].reshape(2 * RIM, WIDTH)
        xh_v[pl.ds(0, 2 * RIM)] = normed(rim.astype(f32))[1]
        edge = dot((east_v if p else west_v)[...], edge1_r[pl.ds(p * SIDE, SIDE)])
        xh_v[pl.ds(2 * RIM, EDGE)] = normed(edge)[1]

        @pl.loop(0, 2 * QUADS, unroll=True)
        def _(c):
            y = dot(xh_v[...], w_v[:, lanes(QUADS + c)])
            rim = y[: 2 * RIM].reshape(2, RADIUS, HALF, QUAD)
            kvx_v[pl.ds(0, RADIUS), pl.ds(p * HALF, HALF), lanes(c)] = rim[0]
            kvx_v[pl.ds(RADIUS + ROWS, RADIUS), pl.ds(p * HALF, HALF), lanes(c)] = rim[1]
            kvx_v[:, pl.ds(COLS + p * TILE, TILE), lanes(c)] = y[2 * RIM :].reshape(
                EXT, TILE, QUAD
            )
            for t in tiles:
                main = kvx_v[:, pl.ds(t * TILE, TILE), lanes(c)]
                east = kvx_v[:, pl.ds((t + 1 if t < TILES - 1 else TILES + 1) * TILE, TILE), lanes(c)]
                west = kvx_v[:, pl.ds((t - 1 if t > 0 else TILES) * TILE, TILE), lanes(c)]
                side = jnp.where(low_side, east, west)
                kt_v[t, :, lanes(c)] = (
                    jnp.concatenate([main, side], axis=1).reshape(SPAN, QUAD).astype(bf16)
                )

    lane_head = lax.broadcasted_iota(jnp.int32, (TILE * ROWS, QUAD), 1) >> 6
    head_masks = [jnp.where(lane_head == h, 1.0, 0.0).astype(bf16) for h in range(4)]

    def stacked(y):
        return jnp.concatenate([y * mask for mask in head_masks], axis=0)

    def unstacked(y):
        n = TILE * ROWS
        out = y[:n]
        for h in range(1, 4):
            out = jnp.where(lane_head == h, y[h * n : (h + 1) * n], out)
        return out.reshape(ROWS, TILE, QUAD)

    chunks = [pl.ds(r, 32) for r in range(0, SPAN, 32)]

    def folded(y):
        return jnp.sum(y.reshape(4, 8, QUAD), axis=0)

    def score(slot, t, j):
        key, value = kt_v[t, :, lanes(j)], kt_v[t, :, lanes(QUADS + j)]
        cells = pl.ds(t * TILE * ROWS, TILE * ROWS)
        query, d_attn = stacked(q_v[cells, lanes(j)]), stacked(da_v[cells, lanes(j)])
        score_v[slot] = dot(key, query, ROWS_BY_ROWS)
        prob_v[slot] = dot(value, d_attn, ROWS_BY_ROWS)

    def weigh(slot, i, t):
        total = jnp.zeros((8, QUAD), f32)
        for rows in chunks:
            mask = mask_v[t, rows]
            terms = jnp.exp(score_v[slot, rows] + jnp.concatenate([mask, mask], axis=1))
            score_v[slot, rows] = terms
            total += folded(terms)
        scale = 1.0 / jnp.sum(total, axis=0, keepdims=True)
        total = jnp.zeros((8, QUAD), f32)
        for rows in chunks:
            weights = score_v[slot, rows] * scale
            weight_v[i, rows] = weights.astype(bf16)
            total += folded(weights * prob_v[slot, rows])
        delta = jnp.sum(total, axis=0, keepdims=True)
        for rows in chunks:
            weights = score_v[slot, rows] * scale
            dscore_v[i, rows] = (weights * (prob_v[slot, rows] - delta)).astype(bf16)

    def to_keys(i, t, j):
        cells = pl.ds(t * TILE * ROWS, TILE * ROWS)
        query, d_attn = stacked(q_v[cells, lanes(j)]), stacked(da_v[cells, lanes(j)])
        dk_v[t, :, :, lanes(j)] = dot(dscore_v[i], query).reshape(EXT, 2 * TILE, QUAD)
        dv_v[t, :, :, lanes(j)] = dot(weight_v[i], d_attn).reshape(EXT, 2 * TILE, QUAD)

    def to_queries(i, t, j):
        key, value = kt_v[t, :, lanes(j)], kt_v[t, :, lanes(QUADS + j)]
        columns = pl.ds(t * TILE, TILE)
        attf_v[:, columns, lanes(j)] = unstacked(dot(weight_v[i].T, value))
        gqf_v[:, columns, lanes(j)] = unstacked(dot(dscore_v[i].T, key)) * (
            HEAD_DIM**-0.5
        )

    def attend(items, before, after):
        for i in range(len(items) + 2):
            if i < len(items):
                before(*items[i])
                score(i % 2, *items[i])
            if 0 <= i - 2:
                to_keys(i - 2, *items[i - 2])
                after(*items[i - 2])
            if 0 <= i - 1 < len(items):
                weigh((i - 1) % 2, i - 1, items[i - 1][0])

    def gathered(j, half, gh_ref):
        for d_ref, block in ((dk_v, j), (dv_v, QUADS + j)):
            groups = []
            for t in (2 * half, 2 * half + 1):
                low = d_ref[t - 1, :, pl.ds(TILE, TILE), lanes(j)] if t > 0 else 0.0
                high = d_ref[t + 1, :, pl.ds(TILE, TILE), lanes(j)] if t < TILES - 1 else 0.0
                main = d_ref[t, :, pl.ds(0, TILE), lanes(j)]
                groups.append(main + jnp.where(low_side, low, high))
            whole = jnp.concatenate(groups, axis=1).astype(bf16)
            g_v[:, pl.ds(half * HALF, HALF), lanes(QUADS + block)] = whole[
                RADIUS : RADIUS + ROWS
            ]
            gh_ref[pl.ds(0, RIM), lanes(block)] = whole[:RADIUS].reshape(RIM, QUAD)
            gh_ref[pl.ds(RIM, RIM), lanes(block)] = whole[RADIUS + ROWS :].reshape(RIM, QUAD)
            if half == 1:
                east = d_ref[TILES - 1, :, pl.ds(TILE, TILE), lanes(j)]
                west = d_ref[0, :, pl.ds(TILE, TILE), lanes(j)]
                edge = jnp.where(low_side, east, west).reshape(EDGE, QUAD).astype(bf16)
                gh_ref[pl.ds(2 * RIM, PACK), lanes(block)] = dot(spreadt_v[...], edge).astype(bf16)

    def projected(gh_ref, out_ref):
        @pl.loop(0, QUADS, unroll=True)
        def _(n):
            y = dot(gh_ref[...], w_v[lanes(n), pl.ds(WIDTH, 2 * WIDTH)], ROWS_BY_ROWS)
            out_ref[:, lanes(n)] = y.astype(bf16)

    n_s = [pl.ds(0, RIM), pl.ds(RIM, RIM)]
    second = rims(
        [send2a_v.at[d] for d in n_s], [recv2a_r.at[d] for d in n_s], 0, send2_sem, recv2_sem
    )
    third = rims(
        [send2b_v.at[d] for d in n_s], [recv2b_r.at[d] for d in n_s], 2, send2_sem, recv2_sem
    ) + pieces(send2b_v, recv2b_r, 2 * RIM, range(6), 4, send2_sem, recv2_sem)

    def before(t, j):
        if (t, j) == (0, 0):
            received(0, (0,))
        if (t, j) == (1, 0):
            received(1, (1, 2, 3))

    def after(t, j):
        if t == 2:
            gathered(j, 0, gh1_v)
        if t == 3:
            gathered(j, 1, gh2_v)
        if (t, j) == (2, QUADS - 1):
            projected(gh1_v, send2a_v)
            for copy in second:
                copy.start()

    items = (
        [(0, j) for j in range(QUADS)]
        + [(t, j) for j in range(QUADS) for t in (1, 2)]
        + [(3, j) for j in range(QUADS)]
    )
    attend(items, before, after)
    projected(gh2_v, send2b_v)
    for copy in third[2:] + third[:2]:
        copy.start()

    for n in range(QUADS):
        for i in range(n * len(items) // QUADS, (n + 1) * len(items) // QUADS):
            to_queries(i, *items[i])
        scaled_o[:, lanes(n)] = dot(
            g_v[:, :, pl.ds(WIDTH, 2 * WIDTH)].reshape(CELLS, 2 * WIDTH),
            w_v[lanes(n), pl.ds(WIDTH, 2 * WIDTH)],
            ROWS_BY_ROWS,
        )
    att_v[...] = attf_v[...].astype(bf16).reshape(CELLS, WIDTH)
    g_v[:, :, pl.ds(0, WIDTH)] = gqf_v[...].astype(bf16)
    for n in range(QUADS):
        mixed_o[:, lanes(n)] = dot(att_v[...], wo_v[:, lanes(n)]).astype(bf16)
        scaled_o[:, lanes(n)] += dot(
            g_v[:, :, pl.ds(0, WIDTH)].reshape(CELLS, WIDTH),
            w_v[lanes(n), pl.ds(0, WIDTH)],
            ROWS_BY_ROWS,
        )

    for copy in second + third:
        copy.wait_recv()

    def both(rows):
        west, east = (r[rows].astype(f32).reshape(RADIUS, HALF, WIDTH) for r in (recv2a_r, recv2b_r))
        return jnp.concatenate([west, east], axis=1).reshape(2 * RIM, WIDTH)

    scaled_o[pl.ds(0, 2 * RIM)] += both(n_s[0])
    scaled_o[pl.ds(CELLS - 2 * RIM, 2 * RIM)] += both(n_s[1])
    edges = dot(packt_v[...], recv2b_r[pl.ds(2 * RIM, PACK)])
    scaled_o[...] = (scaled_o[...] + edges) * gain
    for copy in first[0] + first[1] + second + third:
        copy.wait_send()


def finish(x_ref, mixed_ref, scaled_ref, inv_ref, mixed_hbm, gin_hbm, gin_v, sem):
    mixed_copy = pltpu.make_async_copy(mixed_ref, mixed_hbm, sem.at[0])
    mixed_copy.start()
    blocks = 4
    size = CELLS // blocks
    copies = []
    for b in range(blocks):
        rows = pl.ds(b * size, size)
        x, scaled, inv = x_ref[rows].astype(jnp.float32), scaled_ref[rows], inv_ref[rows][:, :1]
        mean = jnp.mean(x * scaled, axis=-1, keepdims=True)
        gin_v[rows] = (inv * scaled - x * (inv * inv * inv * mean)).astype(gin_v.dtype)
        copies.append(pltpu.make_async_copy(gin_v.at[rows], gin_hbm.at[rows], sem.at[1 + b]))
        copies[-1].start()
    for copy in [mixed_copy] + copies:
        copy.wait()


def shards(inputs, norm_gain, w_qkv, w_out, d_out, corner):
    assert inputs.shape == (ROWS, COLS, WIDTH), inputs.shape
    f32, bf16 = jnp.float32, jnp.bfloat16
    vmem, dma = pltpu.VMEM, pltpu.SemaphoreType.DMA
    anywhere = pl.BlockSpec(memory_space=pl.ANY)
    inside = pl.BlockSpec(memory_space=pltpu.VMEM)
    mixed, scaled, inv = pl.pallas_call(
        kernel,
        out_shape=[
            vmem((CELLS, WIDTH), bf16),
            vmem((CELLS, WIDTH), f32),
            vmem((CELLS, 128), f32),
        ],
        in_specs=[anywhere] * 6,
        out_specs=[inside] * 3,
        scratch_shapes=[
            vmem((ROWS, COLS, WIDTH), bf16),
            vmem((CELLS, WIDTH), bf16),
            vmem((1, WIDTH), f32),
            vmem((ROWS, COLS), jnp.int32),
            vmem((WIDTH, 3 * WIDTH), bf16),
            vmem((WIDTH, WIDTH), bf16),
            vmem((PACK, CELLS), bf16),
            vmem((CELLS, PACK), bf16),
            vmem((EDGE, SIDE), bf16),
            vmem((EDGE, SIDE), bf16),
            vmem((PACK, EDGE), bf16),
            vmem((CELLS, WIDTH), bf16),
            vmem((PART, WIDTH), bf16),
            vmem((CELLS, WIDTH), bf16),
            vmem((CELLS, WIDTH), bf16),
            vmem((EXT, COLS + 2 * TILE, 2 * WIDTH), f32),
            vmem((TILES, SPAN, 2 * WIDTH), bf16),
            vmem((TILES, SPAN, 128), f32),
            vmem((TILES, EXT, 2 * TILE, WIDTH), f32),
            vmem((TILES, EXT, 2 * TILE, WIDTH), f32),
            vmem((ROWS, COLS, WIDTH), f32),
            vmem((ROWS, COLS, WIDTH), f32),
            vmem((CELLS, WIDTH), bf16),
            vmem((ROWS, COLS, 3 * WIDTH), bf16),
            vmem((2 * RIM, 2 * WIDTH), bf16),
            vmem((LATE, 2 * WIDTH), bf16),
            vmem((2, SPAN, QUAD), f32),
            vmem((2, SPAN, QUAD), f32),
            vmem((TILES * QUADS, SPAN, QUAD), bf16),
            vmem((TILES * QUADS, SPAN, QUAD), bf16),
            vmem((PACK, WIDTH), bf16),
            vmem((2 * RADIUS, COLS, WIDTH), bf16),
            vmem((PACK, WIDTH), bf16),
            vmem((2 * RIM, WIDTH), bf16),
            vmem((2 * RIM, WIDTH), bf16),
            vmem((LATE, WIDTH), bf16),
            vmem((LATE, WIDTH), bf16),
            dma((4,)),
            dma((3 * QUADS + 1,)),
            dma((10,)),
            dma((10,)),
            dma((10,)),
            dma((10,)),
        ],
        compiler_params=pltpu.CompilerParams(
            collective_id=0, has_side_effects=True, vmem_limit_bytes=61 * 1024 * 1024
        ),
    )(
        inputs,
        d_out.reshape(CELLS, WIDTH),
        norm_gain.reshape(1, WIDTH),
        corner,
        w_qkv,
        w_out,
    )
    mixed_out, grad_input = pl.pallas_call(
        finish,
        out_shape=[jax.ShapeDtypeStruct((CELLS, WIDTH), bf16)] * 2,
        in_specs=[inside] * 4,
        out_specs=[anywhere] * 2,
        scratch_shapes=[vmem((CELLS, WIDTH), bf16), dma((5,))],
        compiler_params=pltpu.CompilerParams(vmem_limit_bytes=16 * 1024 * 1024),
    )(inputs.reshape(CELLS, WIDTH), mixed, scaled, inv)
    return mixed_out.reshape(inputs.shape), grad_input.reshape(inputs.shape)


def solution(mesh):
    placed = (P("lev", "lon", None), P(), P(), P(), P("lev", "lon", None), P("lev", "lon"))
    return jax.shard_map(
        shards,
        mesh=mesh,
        in_specs=placed,
        out_specs=(P("lev", "lon", None), P("lev", "lon", None)),
        check_vma=False,
    )
```

```python
import jax
import jax.numpy as jnp
from jax import lax
from jax.experimental import pallas as pl
from jax.experimental.pallas import tpu as pltpu
from jax.sharding import PartitionSpec as P

HEADS = 16
RADIUS = 3
EPSILON = 1e-06

ROWS, COLS, WIDTH = 8, 32, 1024
CELLS = ROWS * COLS
HEAD_DIM = WIDTH // HEADS
QUAD = 4 * HEAD_DIM
QUADS = WIDTH // QUAD
TILE = 8
TILES = COLS // TILE
EXT = ROWS + 2 * RADIUS
SPAN = EXT * 2 * TILE
HALF = COLS // 2
RIM = RADIUS * HALF
SIDE = 64
EDGE = EXT * TILE
PACK = 128
PART = 2 * RIM + EDGE
LATE = 2 * RIM + PACK
NEG = -1e30

PIECES = (
    ((0, -1), 0, 32),
    ((-1, -1), 32, 16),
    ((1, -1), 48, 16),
    ((0, 1), 64, 32),
    ((-1, 1), 96, 16),
    ((1, 1), 112, 16),
)
AROUND = ((-1, 0), (1, 0)) + tuple(p[0] for p in PIECES)
OPPOSITE = tuple(AROUND.index((-d[0], -d[1])) for d in AROUND)


def piece_places(p):
    east, r = p >> 6, p & 63
    north, south = (r >= 32) & (r < 48), r >= 48
    i = jnp.where(south, r - 48, jnp.where(north, r - 32, r))
    row = (i * 43) >> 7
    c = i - 3 * row
    valid = row < jnp.where(north | south, RADIUS, ROWS)
    own_row = row + jnp.where(south, ROWS - RADIUS, 0)
    ext_row = row + jnp.where(south, RADIUS + ROWS, jnp.where(north, 0, RADIUS))
    cell = own_row * COLS + c + (COLS - RADIUS) * east
    edge = ext_row * TILE + c + (TILE - RADIUS) * (1 - east)
    return jnp.where(valid, cell, -1), jnp.where(valid, edge, -1)


def selection(shape, axis, which, first=0):
    p = lax.broadcasted_iota(jnp.int32, shape, axis) + first
    other = lax.broadcasted_iota(jnp.int32, shape, 1 - axis)
    return jnp.where(piece_places(p)[which] == other, 1.0, 0.0).astype(jnp.bfloat16)


def dot(a, b, dims=((1,), (0,))):
    return lax.dot_general(a, b, (dims, ((), ())), preferred_element_type=jnp.float32)


ROWS_BY_ROWS = ((1,), (1,))
COLS_BY_COLS = ((0,), (0,))


def lanes(index, size=QUAD):
    if isinstance(index, int):
        return pl.ds(index * size, size)
    return pl.ds(pl.multiple_of(index * size, size), size)


def kernel(
    x_hbm, do_hbm, gain_hbm, corner_hbm, wqkv_hbm, wout_hbm,
    mixed_o, scaled_o, inv_o,
    x_v, do_v, gain_v, corner_v, w_v, wo_v, pack_v, packt_v, west_v, east_v, spreadt_v,
    xn_v, xh_v, q_v, da_v, kvx_v, kt_v, mask_v, dk_v, dv_v,
    attf_v, gqf_v, att_v, g_v, gh1_v, gh2_v,
    score_v, prob_v, weight_v, dscore_v,
    edge1_v, rim1_r, edge1_r, send2a_v, recv2a_r, send2b_v, recv2b_r,
    in_sem, w_sem, send1_sem, recv1_sem, send2_sem, recv2_sem,
):
    f32, bf16 = jnp.float32, jnp.bfloat16
    lon, lev = lax.axis_index("lon"), lax.axis_index("lev")
    lons, levs = lax.axis_size("lon"), lax.axis_size("lev")
    target = [
        {"lon": lax.rem(lon + dx + lons, lons), "lev": lax.rem(lev + dy + levs, levs)}
        for dy, dx in AROUND
    ]
    barrier = pltpu.get_barrier_semaphore()
    for device in target:
        pl.semaphore_signal(
            barrier, inc=1, device_id=device, device_id_type=pl.DeviceIdType.MESH
        )

    small = [
        pltpu.make_async_copy(src, dst, in_sem.at[i])
        for i, (src, dst) in enumerate(
            [
                (x_hbm, x_v), (corner_hbm, corner_v), (gain_hbm, gain_v), (do_hbm, do_v),
            ]
        )
    ]
    for copy in small[:3]:
        copy.start()
    pack_v[...] = selection((PACK, CELLS), 0, 0)

    def weight(c):
        return pltpu.make_async_copy(wqkv_hbm.at[:, lanes(c)], w_v.at[:, lanes(c)], w_sem.at[c])

    out_weight = pltpu.make_async_copy(wout_hbm, wo_v, w_sem.at[3 * QUADS])

    def remote(src, dst, d, slot, send_sem, recv_sem):
        return pltpu.make_async_remote_copy(
            src_ref=src,
            dst_ref=dst,
            send_sem=send_sem.at[slot],
            recv_sem=recv_sem.at[slot],
            device_id=target[d],
            device_id_type=pl.DeviceIdType.MESH,
        )

    def rims(src, dst, slot, send_sem, recv_sem):
        return [
            remote(src[0], dst[1], 0, slot, send_sem, recv_sem),
            remote(src[1], dst[0], 1, slot + 1, send_sem, recv_sem),
        ]

    def pieces(src, dst, base, indices, slot, send_sem, recv_sem):
        copies = []
        for n, i in enumerate(indices):
            at, size = PIECES[i][1:]
            other = PIECES[OPPOSITE[2 + i] - 2][1]
            copies.append(
                remote(
                    src.at[pl.ds(base + at, size)], dst.at[pl.ds(base + other, size)], 2 + i,
                    slot + n, send_sem, recv_sem,
                )
            )
        return copies

    def halves(ref, half):
        columns = pl.ds(half * HALF, HALF)
        return [ref.at[pl.ds(0, RADIUS), columns], ref.at[pl.ds(ROWS - RADIUS, RADIUS), columns]]

    def arrivals(half):
        columns = pl.ds(half * HALF, HALF)
        return [rim1_r.at[pl.ds(0, RADIUS), columns], rim1_r.at[pl.ds(RADIUS, RADIUS), columns]]

    first = [
        rims(halves(x_hbm, p), arrivals(p), 5 * p, send1_sem, recv1_sem)
        + pieces(
            edge1_v, edge1_r, 0, (3, 4, 5) if p == 0 else (0, 1, 2), 5 * p + 2, send1_sem,
            recv1_sem,
        )
        for p in range(2)
    ]
    for c in range(2 * QUADS):
        weight(c).start()
    small[0].wait()
    x_own = x_v[...].reshape(CELLS, WIDTH)
    edge1_v[...] = dot(pack_v[...], x_own).astype(bf16)
    pl.semaphore_wait(barrier, len(target))
    for copy in first[0] + first[1]:
        copy.start()
    for c in range(2 * QUADS, 3 * QUADS):
        weight(c).start()
    small[3].start()
    out_weight.start()
    places = lax.broadcasted_iota(jnp.int32, (PACK, PACK), 0)
    outer = ((places & 63) >> 3) * COLS + (places & 7) + (COLS - TILE) * (places >> 6)
    packed = piece_places(lax.broadcasted_iota(jnp.int32, (PACK, PACK), 1))[0]
    packt_v[...] = jnp.where(packed == outer, 1.0, 0.0).astype(bf16)
    west_v[...] = selection((EDGE, SIDE), 1, 1)
    east_v[...] = selection((EDGE, SIDE), 1, 1, SIDE)
    spreadt_v[...] = selection((PACK, EDGE), 0, 1)

    small[1].wait()
    codes = corner_v[...].astype(f32).astype(bf16)
    key_at = lax.broadcasted_iota(jnp.int32, (SPAN, 128), 0)
    query_at = lax.broadcasted_iota(jnp.int32, (SPAN, 128), 1)
    ext_row, position = key_at >> 4, key_at & 15
    query_row, query_col = (query_at >> 3) & 7, query_at & 7
    key_col = jnp.where(position >= 13, position - 16, position)
    near_row = ext_row - RADIUS - query_row
    near_col = key_col - query_col
    key_row = lev * ROWS + ext_row - RADIUS
    fine = (
        (jnp.abs(near_row) <= RADIUS)
        & (jnp.abs(near_col) <= RADIUS)
        & ((position < 11) | (position > 12))
        & (key_row >= 0)
        & (key_row < levs * ROWS)
    )
    leaves = jnp.where(
        (near_row == 0) | (near_col == 0),
        -1,
        1 + jnp.where(near_row > 0, 2, 0) + jnp.where(near_col > 0, 1, 0),
    ).astype(f32)
    leaves = jnp.where(fine, leaves, -2.0)
    pick_col = lax.broadcasted_iota(jnp.int32, (COLS, 128), 0)
    pick_lane = lax.broadcasted_iota(jnp.int32, (COLS, 128), 1)
    row_of = lax.broadcasted_iota(jnp.int32, (ROWS, 128), 0)
    lane_row = (lax.broadcasted_iota(jnp.int32, (ROWS, 128), 1) >> 3) & 7
    for t in range(TILES):
        pick = jnp.where(pick_col == t * TILE + (pick_lane & 7), 1.0, 0.0).astype(bf16)
        spread_codes = dot(codes, pick)
        code = jnp.sum(
            jnp.where(row_of == lane_row, spread_codes, 0.0), axis=0, keepdims=True
        )
        mask_v[t] = jnp.where((leaves == code) | (leaves < -1.5), NEG, 0.0)

    small[2].wait()
    gain = gain_v[...]

    def normed(x):
        inv = lax.rsqrt(jnp.mean(x * x, axis=-1, keepdims=True) + EPSILON)
        return inv, (x * inv * gain).astype(bf16)

    inv_own, own = normed(x_own.astype(f32))
    xn_v[...] = own
    inv_o[...] = jnp.broadcast_to(inv_own, (CELLS, 128))

    def by_tiles(y):
        y = y.reshape(ROWS, TILES, TILE, QUAD)
        return jnp.concatenate([y[:, t] for t in range(TILES)], axis=0).reshape(CELLS, QUAD)

    for c in range(QUADS):
        weight(c).wait()
    for c in range(QUADS):
        y = dot(xn_v[...], w_v[:, lanes(c)]) * (HEAD_DIM**-0.5)
        q_v[:, lanes(c)] = by_tiles(y).astype(bf16)

    for c in range(QUADS, 3 * QUADS):
        weight(c).wait()
    for c in range(2 * QUADS):
        y = dot(xn_v[...], w_v[:, lanes(QUADS + c)])
        kvx_v[pl.ds(RADIUS, ROWS), pl.ds(0, COLS), lanes(c)] = y.reshape(ROWS, COLS, QUAD)

    small[3].wait()
    out_weight.wait()

    @pl.loop(0, QUADS, unroll=True)
    def _(c):
        y = dot(do_v[...], wo_v[lanes(c), :], ROWS_BY_ROWS)
        da_v[:, lanes(c)] = by_tiles(y).astype(bf16)

    low_side = lax.broadcasted_iota(jnp.int32, (EXT, TILE, QUAD), 1) < 4

    def received(p, tiles):
        for copy in first[p]:
            copy.wait_recv()
        rim = rim1_r[:, pl.ds(p * HALF, HALF)].reshape(2 * RIM, WIDTH)
        xh_v[pl.ds(0, 2 * RIM)] = normed(rim.astype(f32))[1]
        edge = dot((east_v if p else west_v)[...], edge1_r[pl.ds(p * SIDE, SIDE)])
        xh_v[pl.ds(2 * RIM, EDGE)] = normed(edge)[1]

        @pl.loop(0, 2 * QUADS, unroll=True)
        def _(c):
            y = dot(xh_v[...], w_v[:, lanes(QUADS + c)])
            rim = y[: 2 * RIM].reshape(2, RADIUS, HALF, QUAD)
            kvx_v[pl.ds(0, RADIUS), pl.ds(p * HALF, HALF), lanes(c)] = rim[0]
            kvx_v[pl.ds(RADIUS + ROWS, RADIUS), pl.ds(p * HALF, HALF), lanes(c)] = rim[1]
            kvx_v[:, pl.ds(COLS + p * TILE, TILE), lanes(c)] = y[2 * RIM :].reshape(
                EXT, TILE, QUAD
            )
            for t in tiles:
                main = kvx_v[:, pl.ds(t * TILE, TILE), lanes(c)]
                east = kvx_v[:, pl.ds((t + 1 if t < TILES - 1 else TILES + 1) * TILE, TILE), lanes(c)]
                west = kvx_v[:, pl.ds((t - 1 if t > 0 else TILES) * TILE, TILE), lanes(c)]
                side = jnp.where(low_side, east, west)
                kt_v[t, :, lanes(c)] = (
                    jnp.concatenate([main, side], axis=1).reshape(SPAN, QUAD).astype(bf16)
                )

    lane_head = lax.broadcasted_iota(jnp.int32, (TILE * ROWS, QUAD), 1) >> 6
    head_masks = [jnp.where(lane_head == h, 1.0, 0.0).astype(bf16) for h in range(4)]

    def stacked(y):
        return jnp.concatenate([y * mask for mask in head_masks], axis=0)

    def unstacked(y):
        n = TILE * ROWS
        out = y[:n]
        for h in range(1, 4):
            out = jnp.where(lane_head == h, y[h * n : (h + 1) * n], out)
        return out.reshape(ROWS, TILE, QUAD)

    chunks = [pl.ds(r, 32) for r in range(0, SPAN, 32)]

    def folded(y):
        return jnp.sum(y.reshape(4, 8, QUAD), axis=0)

    def score(slot, t, j):
        key, value = kt_v[t, :, lanes(j)], kt_v[t, :, lanes(QUADS + j)]
        cells = pl.ds(t * TILE * ROWS, TILE * ROWS)
        query, d_attn = stacked(q_v[cells, lanes(j)]), stacked(da_v[cells, lanes(j)])
        score_v[slot] = dot(key, query, ROWS_BY_ROWS)
        prob_v[slot] = dot(value, d_attn, ROWS_BY_ROWS)

    def weigh(slot, i, t):
        total = jnp.zeros((8, QUAD), f32)
        for rows in chunks:
            mask = mask_v[t, rows]
            terms = jnp.exp(score_v[slot, rows] + jnp.concatenate([mask, mask], axis=1))
            score_v[slot, rows] = terms
            total += folded(terms)
        scale = 1.0 / jnp.sum(total, axis=0, keepdims=True)
        total = jnp.zeros((8, QUAD), f32)
        for rows in chunks:
            weights = score_v[slot, rows] * scale
            weight_v[i, rows] = weights.astype(bf16)
            total += folded(weights * prob_v[slot, rows])
        delta = jnp.sum(total, axis=0, keepdims=True)
        for rows in chunks:
            weights = score_v[slot, rows] * scale
            dscore_v[i, rows] = (weights * (prob_v[slot, rows] - delta)).astype(bf16)

    def to_keys(i, t, j):
        cells = pl.ds(t * TILE * ROWS, TILE * ROWS)
        query, d_attn = stacked(q_v[cells, lanes(j)]), stacked(da_v[cells, lanes(j)])
        dk_v[t, :, :, lanes(j)] = dot(dscore_v[i], query).reshape(EXT, 2 * TILE, QUAD)
        dv_v[t, :, :, lanes(j)] = dot(weight_v[i], d_attn).reshape(EXT, 2 * TILE, QUAD)

    def to_queries(i, t, j):
        key, value = kt_v[t, :, lanes(j)], kt_v[t, :, lanes(QUADS + j)]
        columns = pl.ds(t * TILE, TILE)
        attf_v[:, columns, lanes(j)] = unstacked(dot(weight_v[i].T, value))
        gqf_v[:, columns, lanes(j)] = unstacked(dot(dscore_v[i].T, key)) * (
            HEAD_DIM**-0.5
        )

    def attend(items, before, after):
        for i in range(len(items) + 2):
            if i < len(items):
                before(*items[i])
                score(i % 2, *items[i])
            if 0 <= i - 2:
                to_keys(i - 2, *items[i - 2])
                after(*items[i - 2])
            if 0 <= i - 1 < len(items):
                weigh((i - 1) % 2, i - 1, items[i - 1][0])

    def gathered(j, half, gh_ref):
        for d_ref, block in ((dk_v, j), (dv_v, QUADS + j)):
            groups = []
            for t in (2 * half, 2 * half + 1):
                low = d_ref[t - 1, :, pl.ds(TILE, TILE), lanes(j)] if t > 0 else 0.0
                high = d_ref[t + 1, :, pl.ds(TILE, TILE), lanes(j)] if t < TILES - 1 else 0.0
                main = d_ref[t, :, pl.ds(0, TILE), lanes(j)]
                groups.append(main + jnp.where(low_side, low, high))
            whole = jnp.concatenate(groups, axis=1).astype(bf16)
            g_v[:, pl.ds(half * HALF, HALF), lanes(QUADS + block)] = whole[
                RADIUS : RADIUS + ROWS
            ]
            gh_ref[pl.ds(0, RIM), lanes(block)] = whole[:RADIUS].reshape(RIM, QUAD)
            gh_ref[pl.ds(RIM, RIM), lanes(block)] = whole[RADIUS + ROWS :].reshape(RIM, QUAD)
            if half == 1:
                east = d_ref[TILES - 1, :, pl.ds(TILE, TILE), lanes(j)]
                west = d_ref[0, :, pl.ds(TILE, TILE), lanes(j)]
                edge = jnp.where(low_side, east, west).reshape(EDGE, QUAD).astype(bf16)
                gh_ref[pl.ds(2 * RIM, PACK), lanes(block)] = dot(spreadt_v[...], edge).astype(bf16)

    def projected(gh_ref, out_ref):
        @pl.loop(0, QUADS, unroll=True)
        def _(n):
            y = dot(gh_ref[...], w_v[lanes(n), pl.ds(WIDTH, 2 * WIDTH)], ROWS_BY_ROWS)
            out_ref[:, lanes(n)] = y.astype(bf16)

    n_s = [pl.ds(0, RIM), pl.ds(RIM, RIM)]
    second = rims(
        [send2a_v.at[d] for d in n_s], [recv2a_r.at[d] for d in n_s], 0, send2_sem, recv2_sem
    )
    third = rims(
        [send2b_v.at[d] for d in n_s], [recv2b_r.at[d] for d in n_s], 2, send2_sem, recv2_sem
    ) + pieces(send2b_v, recv2b_r, 2 * RIM, range(6), 4, send2_sem, recv2_sem)

    def before(t, j):
        if (t, j) == (0, 0):
            received(0, (0,))
        if (t, j) == (1, 0):
            received(1, (1, 2, 3))

    def after(t, j):
        if t == 2:
            gathered(j, 0, gh1_v)
        if t == 3:
            gathered(j, 1, gh2_v)
        if (t, j) == (2, QUADS - 1):
            projected(gh1_v, send2a_v)
            for copy in second:
                copy.start()

    items = (
        [(0, j) for j in range(QUADS)]
        + [(t, j) for j in range(QUADS) for t in (1, 2)]
        + [(3, j) for j in range(QUADS)]
    )
    attend(items, before, after)
    projected(gh2_v, send2b_v)
    for copy in third[2:] + third[:2]:
        copy.start()

    for n in range(QUADS):
        for i in range(n * len(items) // QUADS, (n + 1) * len(items) // QUADS):
            to_queries(i, *items[i])
        scaled_o[:, lanes(n)] = dot(
            g_v[:, :, pl.ds(WIDTH, 2 * WIDTH)].reshape(CELLS, 2 * WIDTH),
            w_v[lanes(n), pl.ds(WIDTH, 2 * WIDTH)],
            ROWS_BY_ROWS,
        )
    att_v[...] = attf_v[...].astype(bf16).reshape(CELLS, WIDTH)
    g_v[:, :, pl.ds(0, WIDTH)] = gqf_v[...].astype(bf16)
    for n in range(QUADS):
        mixed_o[:, lanes(n)] = dot(att_v[...], wo_v[:, lanes(n)]).astype(bf16)
        own = dot(
            g_v[:, :, pl.ds(0, WIDTH)].reshape(CELLS, WIDTH),
            w_v[lanes(n), pl.ds(0, WIDTH)],
            ROWS_BY_ROWS,
        )
        scaled_o[:, lanes(n)] = (scaled_o[:, lanes(n)] + own) * gain_v[:, lanes(n)]

    def add_rims(ref, half):
        for i, top in enumerate((0, ROWS - RADIUS)):
            y = ref[n_s[i]].astype(f32) * gain
            for r in range(RADIUS):
                cells = pl.ds((top + r) * COLS + half * HALF, HALF)
                scaled_o[cells] += y[r * HALF : (r + 1) * HALF]

    for copy in second:
        copy.wait_recv()
    add_rims(recv2a_r, 0)
    for copy in third:
        copy.wait_recv()
    add_rims(recv2b_r, 1)
    edges = dot(packt_v[...], recv2b_r[pl.ds(2 * RIM, PACK)]) * gain
    for side in range(2):
        for r in range(ROWS):
            cells = pl.ds(r * COLS + side * (COLS - TILE), TILE)
            at = side * SIDE + r * TILE
            scaled_o[cells] += edges[at : at + TILE]
    for copy in first[0] + first[1] + second + third:
        copy.wait_send()


def finish(x_ref, mixed_ref, scaled_ref, inv_ref, mixed_hbm, gin_hbm, gin_v, sem):
    mixed_copy = pltpu.make_async_copy(mixed_ref, mixed_hbm, sem.at[0])
    mixed_copy.start()
    blocks = 4
    size = CELLS // blocks
    copies = []
    for b in range(blocks):
        rows = pl.ds(b * size, size)
        x, scaled, inv = x_ref[rows].astype(jnp.float32), scaled_ref[rows], inv_ref[rows][:, :1]
        mean = jnp.mean(x * scaled, axis=-1, keepdims=True)
        gin_v[rows] = (inv * scaled - x * (inv * inv * inv * mean)).astype(gin_v.dtype)
        copies.append(pltpu.make_async_copy(gin_v.at[rows], gin_hbm.at[rows], sem.at[1 + b]))
        copies[-1].start()
    for copy in [mixed_copy] + copies:
        copy.wait()


def shards(inputs, norm_gain, w_qkv, w_out, d_out, corner):
    assert inputs.shape == (ROWS, COLS, WIDTH), inputs.shape
    f32, bf16 = jnp.float32, jnp.bfloat16
    vmem, dma = pltpu.VMEM, pltpu.SemaphoreType.DMA
    anywhere = pl.BlockSpec(memory_space=pl.ANY)
    inside = pl.BlockSpec(memory_space=pltpu.VMEM)
    mixed, scaled, inv = pl.pallas_call(
        kernel,
        out_shape=[
            vmem((CELLS, WIDTH), bf16),
            vmem((CELLS, WIDTH), f32),
            vmem((CELLS, 128), f32),
        ],
        in_specs=[anywhere] * 6,
        out_specs=[inside] * 3,
        scratch_shapes=[
            vmem((ROWS, COLS, WIDTH), bf16),
            vmem((CELLS, WIDTH), bf16),
            vmem((1, WIDTH), f32),
            vmem((ROWS, COLS), jnp.int32),
            vmem((WIDTH, 3 * WIDTH), bf16),
            vmem((WIDTH, WIDTH), bf16),
            vmem((PACK, CELLS), bf16),
            vmem((PACK, PACK), bf16),
            vmem((EDGE, SIDE), bf16),
            vmem((EDGE, SIDE), bf16),
            vmem((PACK, EDGE), bf16),
            vmem((CELLS, WIDTH), bf16),
            vmem((PART, WIDTH), bf16),
            vmem((CELLS, WIDTH), bf16),
            vmem((CELLS, WIDTH), bf16),
            vmem((EXT, COLS + 2 * TILE, 2 * WIDTH), f32),
            vmem((TILES, SPAN, 2 * WIDTH), bf16),
            vmem((TILES, SPAN, 128), f32),
            vmem((TILES, EXT, 2 * TILE, WIDTH), f32),
            vmem((TILES, EXT, 2 * TILE, WIDTH), f32),
            vmem((ROWS, COLS, WIDTH), f32),
            vmem((ROWS, COLS, WIDTH), f32),
            vmem((CELLS, WIDTH), bf16),
            vmem((ROWS, COLS, 3 * WIDTH), bf16),
            vmem((2 * RIM, 2 * WIDTH), bf16),
            vmem((LATE, 2 * WIDTH), bf16),
            vmem((2, SPAN, QUAD), f32),
            vmem((2, SPAN, QUAD), f32),
            vmem((TILES * QUADS, SPAN, QUAD), bf16),
            vmem((TILES * QUADS, SPAN, QUAD), bf16),
            vmem((PACK, WIDTH), bf16),
            vmem((2 * RADIUS, COLS, WIDTH), bf16),
            vmem((PACK, WIDTH), bf16),
            vmem((2 * RIM, WIDTH), bf16),
            vmem((2 * RIM, WIDTH), bf16),
            vmem((LATE, WIDTH), bf16),
            vmem((LATE, WIDTH), bf16),
            dma((4,)),
            dma((3 * QUADS + 1,)),
            dma((10,)),
            dma((10,)),
            dma((10,)),
            dma((10,)),
        ],
        compiler_params=pltpu.CompilerParams(
            collective_id=0, has_side_effects=True, vmem_limit_bytes=61 * 1024 * 1024
        ),
    )(
        inputs,
        d_out.reshape(CELLS, WIDTH),
        norm_gain.reshape(1, WIDTH),
        corner,
        w_qkv,
        w_out,
    )
    mixed_out, grad_input = pl.pallas_call(
        finish,
        out_shape=[jax.ShapeDtypeStruct((CELLS, WIDTH), bf16)] * 2,
        in_specs=[inside] * 4,
        out_specs=[anywhere] * 2,
        scratch_shapes=[vmem((CELLS, WIDTH), bf16), dma((5,))],
        compiler_params=pltpu.CompilerParams(vmem_limit_bytes=16 * 1024 * 1024),
    )(inputs.reshape(CELLS, WIDTH), mixed, scaled, inv)
    return mixed_out.reshape(inputs.shape), grad_input.reshape(inputs.shape)


def solution(mesh):
    placed = (P("lev", "lon", None), P(), P(), P(), P("lev", "lon", None), P("lev", "lon"))
    return jax.shard_map(
        shards,
        mesh=mesh,
        in_specs=placed,
        out_specs=(P("lev", "lon", None), P("lev", "lon", None)),
        check_vma=False,
    )
```
